768 devices in a mesh: lon: 24 (over z_lo, x), lat: 16 (over y, core), section: 2 (over z_hi).
Axes of the slice: x: 4, y: 8, z: 12 (z_hi: 2, z_lo: 6; z = z_hi * 6 + z_lo), core: 2. Of those that a mesh axis runs over, the one named last changes fastest.
Arguments:
- inputs: bfloat16 [2, 4, 96, 288, 320], P('section', None, 'lat', 'lon'), may hold values from -6 to 6
- ln_gain: bfloat16 [2, 2, 320], P('section'), may hold values from 0.099609375 to 1.8984375
- ln_shift: bfloat16 [2, 2, 320], P('section'), may hold values from -3 to 3
- qkv_weight: bfloat16 [2, 320, 960], P('section')
- qkv_bias: bfloat16 [2, 960], P('section'), may hold values from -2 to 2
- proj_weight: bfloat16 [2, 320, 320], P('section'), may hold values from -0.3125 to 0.3125
- fc1_weight: bfloat16 [2, 320, 1280], P('section'), may hold values from -0.3125 to 0.3125
- fc1_bias: bfloat16 [2, 1280], P('section'), may hold values from -2 to 2
- fc2_weight: bfloat16 [2, 1280, 320], P('section'), may hold values from -0.15625 to 0.15625
- out_bias: bfloat16 [2, 2, 320], P('section'), may hold values from -2 to 2
- bias_table: bfloat16 [2, 2, 16, 10, 3312], P('section', None, 'lat'), may hold values from -5 to 5
Outputs:
- result: bfloat16 [2, 4, 96, 288, 320], P('section', None, 'lat', 'lon')
The draws below stay inside these ranges and needn't reach their ends.
All inputs are finite; a program needn't handle non-finite values.
Results may differ from the reference program's by a relative error of at most 0.012.
The reference program's roundings to bfloat16 on the way count: a program that leaves them out, or rounds other values in their place, can miss the bound.
Values may be sent and summed in bfloat16 or wider, within the bound.
No kernel may reach another device: no remote copies, remote signals or barrier semaphores. Data moves between devices by JAX's collectives and lax.ppermute only.
A program may use at most 128 MiB of HBM per device.

```python
import jax
import jax.numpy as jnp
import numpy as np
from jax import lax

C = 320
HD = 32
HEADS = 10
FF = 1280
LEV = 4
WLEV = 2
WLAT = 6
WLON = 12
NLAT = 96
NLON = 288
NMB = 2
LEVW = 2
NLATW = 16
POS = 3312


def draw_qkv_weight(key, part):
    key_query, key_key, key_value = jax.random.split(key, 3)
    factor = C ** (-0.5)
    queries = jax.random.normal(key_query, (2, C, C), jnp.float32) * factor
    value_part = jax.random.normal(key_value, (2, C, C), jnp.float32) * factor
    key_part = jax.random.normal(key_key, (2, C, C), jnp.float32) * factor
    return jnp.concatenate([queries, key_part, value_part], axis=2).astype(jnp.bfloat16)


def block_scale(rng, extent, cuts, least, high):
    factor_of = 1.0
    for axis_at, parts in cuts:
        draws = jax.random.uniform(jax.random.fold_in(jax.random.fold_in(rng, 6), axis_at), (parts,), jnp.float32, least / len(cuts), high / len(cuts))
        factor_of = factor_of * jnp.repeat(jnp.exp(draws), extent[axis_at] // parts).reshape((-1,) + (1,) * (len(extent) - 1 - axis_at))
    return factor_of


def scatter_about(rng, shape, deviation, reach, cuts=(), held_as=jnp.bfloat16):
    gain = block_scale(rng, shape, cuts, -0.22, 0.18) if cuts else 1.0
    result = jax.random.normal(rng, shape, jnp.float32) * deviation * gain
    return jnp.minimum(jnp.maximum(result, -reach), reach).astype(held_as)


def setup_inputs(seed: int = 0) -> dict:
    seeds = jax.random.split(jax.random.key(seed), 12)
    inputs = scatter_about(seeds[0], (NMB, LEV, NLAT, NLON, C), 1.0, 6.0, ((0, 2), (2, 16), (3, 24)))
    ln_gain = jnp.clip(1.0 + 0.18 * jax.random.normal(seeds[1], (2, 2, C), jnp.float32), 0.099609375, 1.8984375).astype(jnp.bfloat16)
    ln_shift = scatter_about(seeds[2], (2, 2, C), 0.5, 3.0, ((0, 2),))
    qkv_weight = draw_qkv_weight(jax.random.fold_in(seeds[11], 71), 0)
    qkv_bias = scatter_about(seeds[4], (2, 3 * C), 0.3, 2.0, ((0, 2),))
    proj_weight = scatter_about(seeds[5], (2, C, C), C ** -0.5, 0.3125, ((0, 2),))
    fc1_weight = scatter_about(seeds[6], (2, C, FF), C ** -0.5, 0.3125, ((0, 2),))
    fc1_bias = scatter_about(seeds[7], (2, FF), 0.3, 2.0, ((0, 2),))
    fc2_weight = scatter_about(seeds[8], (2, FF, C), FF ** -0.5, 0.15625, ((0, 2),))
    out_bias = scatter_about(seeds[9], (2, 2, C), 0.3, 2.0, ((0, 2),))
    bias_table = scatter_about(seeds[10], (2, LEVW, NLATW, HEADS, POS), 1.0, 5.0, ((0, 2), (2, 16)))
    return dict(inputs=inputs, ln_gain=ln_gain, ln_shift=ln_shift, qkv_weight=qkv_weight, qkv_bias=qkv_bias, proj_weight=proj_weight, fc1_weight=fc1_weight, fc1_bias=fc1_bias, fc2_weight=fc2_weight, out_bias=out_bias, bias_table=bias_table)


def pair_index():
    lev_pos, lat_pos, lon_pos = np.meshgrid(np.arange(WLEV), np.arange(WLAT), np.arange(WLON), indexing='ij')
    lev_pos = lev_pos.reshape(-1)
    lat_pos = lat_pos.reshape(-1)
    lon_pos = lon_pos.reshape(-1)
    pair_ids = (lev_pos[:, None] + lev_pos[None, :] * WLEV) * (WLAT * WLAT * (2 * WLON - 1))
    pair_ids = pair_ids + (lat_pos[:, None] + lat_pos[None, :] * WLAT) * (2 * WLON - 1)
    pair_ids = pair_ids + lon_pos[:, None] - lon_pos[None, :] + WLON - 1
    return pair_ids.reshape(-1).astype(np.int32)

def layer_norm(values, norm_gain, norm_shift):
    center = values - lax.optimization_barrier(jnp.mean(values, axis=-1, keepdims=True))
    spread = lax.optimization_barrier(jnp.mean(center * center, axis=-1, keepdims=True))
    return center * lax.rsqrt(spread + 1e-05) * norm_gain.astype(jnp.float32) + norm_shift.astype(jnp.float32)

def to_windows(field_grid):
    levels, lat_cells, lon_cells, channels = field_grid.shape
    field_grid = field_grid.reshape(levels // WLEV, WLEV, lat_cells // WLAT, WLAT, lon_cells // WLON, WLON, channels)
    field_grid = field_grid.transpose(0, 2, 4, 1, 3, 5, 6)
    return field_grid.reshape(levels // WLEV, lat_cells // WLAT, lon_cells // WLON, WLEV * WLAT * WLON, channels)

def from_windows(windows, levels, lat_cells, lon_cells):
    channels = windows.shape[-1]
    field_grid = windows.reshape(levels // WLEV, lat_cells // WLAT, lon_cells // WLON, WLEV, WLAT, WLON, channels)
    field_grid = field_grid.transpose(0, 3, 1, 4, 2, 5, 6)
    return field_grid.reshape(levels, lat_cells, lon_cells, channels)

def attend(windows, qkv_w, qkv_b, bias_dense, groups):
    channels = windows.shape[-1]
    head_count = channels // HD
    leading = windows.shape[:4]
    packed = jnp.einsum('abcnd,de->abcne', windows.astype(jnp.float32), qkv_w.astype(jnp.float32))
    packed = (packed + qkv_b.astype(jnp.float32)).astype(jnp.bfloat16)
    queries = packed[..., :channels].reshape(leading + (head_count, HD)).astype(jnp.float32)
    key_rows = packed[..., channels:2 * channels].reshape(leading + (head_count, HD)).astype(jnp.float32)
    values = packed[..., 2 * channels:].reshape(leading + (head_count, HD)).astype(jnp.float32)
    scores = jnp.einsum('abcnhd,abcmhd->abchnm', queries, key_rows) * HD ** (-0.5)
    scores = scores + bias_dense[:, :, None]
    allowed = groups[:, :, None, None, :, None] == groups[:, :, None, None, None, :]
    scores = jnp.where(allowed, scores, -1e+30)
    row_peak = lax.optimization_barrier(jnp.max(scores, axis=-1, keepdims=True))
    raised = jnp.exp(scores - row_peak)
    weights_bf = (raised / lax.optimization_barrier(jnp.sum(raised, axis=-1, keepdims=True))).astype(jnp.bfloat16)
    mixed = jnp.einsum('abchnm,abcmhd->abcnhd', weights_bf.astype(jnp.float32), values)
    return mixed.astype(jnp.bfloat16).reshape(leading + (channels,))

def apply_block(field, params, shifted):
    ln_g, ln_s, qkv_w, qkv_b, proj_w, fc1_w, fc1_b, fc2_w, out_b, table = params
    levels, lat_cells, lon_cells, channels = field.shape
    if shifted:
        lev_off, lat_off, lon_off = (WLEV // 2, WLAT // 2, WLON // 2)
    else:
        lev_off, lat_off, lon_off = (0, 0, 0)
    field_wide = field.astype(jnp.float32)
    normed = layer_norm(field_wide, ln_g[0], ln_s[0]).astype(jnp.bfloat16)
    rolled = jnp.roll(normed, (-lev_off, -lat_off, -lon_off), axis=(0, 1, 2))
    windows = to_windows(rolled)
    lev_flag = (jnp.arange(levels) + lev_off >= levels).astype(jnp.int32)
    lat_flag = (jnp.arange(lat_cells) + lat_off >= lat_cells).astype(jnp.int32)
    group_grid = jnp.broadcast_to(lev_flag[:, None, None] * 2 + lat_flag[None, :, None], (levels, lat_cells, WLON))
    groups = to_windows(group_grid[..., None])[:, :, 0, :, 0]
    pair_ids = jnp.asarray(pair_index())
    win_count = WLEV * WLAT * WLON

    def per_band(pieces):
        band_windows, band_table, band_groups = pieces
        dense = jnp.take(band_table, pair_ids, axis=2).astype(jnp.float32)
        dense = dense.reshape(band_table.shape[0], band_table.shape[1], win_count, win_count)
        mixed = attend(band_windows[:, None], qkv_w, qkv_b, dense[:, None], band_groups[:, None])
        return mixed[:, 0]
    banded = lax.map(per_band, (windows.transpose(1, 0, 2, 3, 4), table.transpose(1, 0, 2, 3), groups.transpose(1, 0, 2)))
    attended = from_windows(banded.transpose(1, 0, 2, 3, 4), levels, lat_cells, lon_cells)
    attended = jnp.roll(attended, (lev_off, lat_off, lon_off), axis=(0, 1, 2))
    flat_att = attended.reshape(-1, channels)
    mid = field_wide.reshape(-1, channels) + jnp.dot(flat_att, proj_w, preferred_element_type=jnp.float32) + out_b[0].astype(jnp.float32)
    normed_two = layer_norm(mid, ln_g[1], ln_s[1]).astype(jnp.bfloat16)
    hidden = jax.nn.gelu(jnp.dot(normed_two, fc1_w, preferred_element_type=jnp.float32) + fc1_b.astype(jnp.float32), approximate=False).astype(jnp.bfloat16)
    outcome = mid + jnp.dot(hidden, fc2_w, preferred_element_type=jnp.float32) + out_b[1].astype(jnp.float32)
    return outcome.astype(jnp.bfloat16).reshape(levels, lat_cells, lon_cells, channels)

def reference(inputs, ln_gain, ln_shift, qkv_weight, qkv_bias, proj_weight, fc1_weight, fc1_bias, fc2_weight, out_bias, bias_table):
    stacked = (ln_gain, ln_shift, qkv_weight, qkv_bias, proj_weight, fc1_weight, fc1_bias, fc2_weight, out_bias, bias_table)
    first_params = tuple((member[0] for member in stacked))
    second_params = tuple((member[1] for member in stacked))
    outputs = []
    for sample in range(NMB):
        middle = apply_block(inputs[sample], first_params, False)
        outputs.append(apply_block(middle, second_params, True))
    return jnp.stack(outputs, axis=0)
```

```python
import functools

import jax
import jax.numpy as jnp
import numpy as np
from jax import lax
from jax.experimental import pallas as pl
from jax.experimental.pallas import tpu as pltpu
from jax.sharding import PartitionSpec as P

HD = 32
HEADS = 10
C = 320
WLEV = 2
WLAT = 6
WLON = 12
WIN = WLEV * WLAT * WLON
QUARTER = WIN // 4
PIECE = QUARTER // WLEV
SPAN = 2 * WLON - 1
AXES = ("lon", "lat", "section")
VMEM_LIMIT = 20 * 1024 * 1024


def token_row(lev, lat, lon):
    quarter = (lat // 3) * 2 + lon // 6
    return quarter * QUARTER + lev * PIECE + (lat % 3) * 6 + lon % 6


def spread_matrix():
    spread = np.zeros((WLEV * WLAT * SPAN, WLON, 256), np.float32)
    for lev in range(WLEV):
        for lat in range(WLAT):
            for lon in range(WLON):
                for query_lon in range(WLON):
                    source = (lev * WLAT + lat) * SPAN + query_lon - lon + WLON - 1
                    spread[source, query_lon, token_row(lev, lat, lon)] = 1.0
    return spread.reshape(WLEV * WLAT * SPAN, WLON * 256).astype(jnp.bfloat16)


def arrange_matrix():
    arrange = np.zeros((2 * WIN, 2 * WIN), np.float32)
    for lev in range(4):
        for lat in range(WLAT):
            for lon in range(WLON):
                row = (lev // 2) * WIN + token_row(lev % 2, lat, lon)
                arrange[row, (lat * WLON + lon) * 4 + lev] = 1.0
    return arrange.astype(jnp.bfloat16)


def place_matrix():
    arrange = np.zeros((2 * WIN, 2 * WIN), np.float32)
    for lev in range(4):
        for lat in range(WLAT):
            for lon in range(WLON):
                quarter = (lat // 3) * 2 + lon // 6
                source = ((quarter * 4 + (lev + 3) % 4) * 3 + lat % 3) * 6 + lon % 6
                arrange[(lat * WLON + lon) * 4 + lev, source] = 1.0
    return arrange.astype(jnp.bfloat16)


def prepare_kernel(table_ref, spread_ref, addend_ref, wide_ref):
    section = lax.axis_index("section")
    last_lat = lax.axis_index("lat") == lax.axis_size("lat") - 1
    wide_ref[0:HEADS, :] = table_ref[0, 0, 0].astype(jnp.float32)
    wide_ref[16 : 16 + HEADS, :] = table_ref[0, 1, 0].astype(jnp.float32)
    for lev in range(WLEV):
        for lat in range(WLAT):
            parts = []
            for key_lev in range(WLEV):
                for key_lat in range(WLAT):
                    at = ((key_lev * WLEV + lev) * WLAT * WLAT + key_lat * WLAT + lat) * SPAN
                    parts.append(wide_ref[:, at : at + SPAN])
            rows = jnp.concatenate(parts, axis=1).astype(jnp.bfloat16)
            dense = jnp.dot(rows, spread_ref[...], preferred_element_type=jnp.float32)
            for lon in range(WLON):
                row = token_row(lev, lat, lon)
                for window in range(2):
                    for tile in range(2):
                        lanes = lon * 256 + tile * 128
                        addend_ref[
                            tile, pl.ds(window * HEADS * WIN + row, HEADS, stride=WIN), :
                        ] = dense[window * 16 : window * 16 + HEADS, lanes : lanes + 128]

    @pl.when(section == 1)
    def mask():
        for tile in range(2):
            query = lax.broadcasted_iota(jnp.int32, (WIN, 128), 0)
            key = lax.broadcasted_iota(jnp.int32, (WIN, 128), 1) + tile * 128
            lat_differs = jnp.logical_and((query >= 2 * QUARTER) != (key >= 2 * QUARTER), last_lat)
            lev_differs = (query % QUARTER >= PIECE) != (key % QUARTER >= PIECE)
            for window in range(2):
                barred = jnp.logical_or(lat_differs, lev_differs) if window else lat_differs
                for head in range(HEADS):
                    at = (window * HEADS + head) * WIN
                    addend_ref[tile, at : at + WIN, :] = jnp.where(
                        barred, jnp.float32(-1e30), addend_ref[tile, at : at + WIN, :]
                    )


def layer_norm(values, norm_gain, norm_shift):
    center = values - jnp.mean(values, axis=-1, keepdims=True)
    spread = jnp.mean(center * center, axis=-1, keepdims=True)
    return center * lax.rsqrt(spread + 1e-05) * norm_gain.astype(jnp.float32) + norm_shift.astype(
        jnp.float32
    )


def run_block(field_ref, params, addend_ref, packed_ref, attended_ref):
    ln_g, ln_s, qkv_w, qkv_b, proj_w, fc1_w, fc1_b, fc2_w, out_b = params
    normed = layer_norm(field_ref[...], ln_g[0, 0:1], ln_s[0, 0:1]).astype(jnp.bfloat16)
    packed = jnp.dot(normed, qkv_w[0], preferred_element_type=jnp.float32)
    packed = (packed + qkv_b[...].astype(jnp.float32)).astype(jnp.bfloat16)
    packed_ref[:, 0:C] = packed[:, 0:C]
    packed_ref[:, 384 : 384 + C] = packed[:, C : 2 * C]
    packed_ref[:, 768 : 768 + C] = packed[:, 2 * C :]
    for window in range(2):
        first = window * WIN
        for group in range(3):
            width = 128 if group < 2 else 64
            heads = width // HD
            lanes = group * 128
            queries = packed_ref[first : first + WIN, lanes : lanes + width]
            keys = packed_ref[first : first + WIN, 384 + lanes : 384 + lanes + width]
            values = packed_ref[first : first + WIN, 768 + lanes : 768 + lanes + width]
            lane_head = lax.broadcasted_iota(jnp.int32, (WIN, width), 1) // HD
            ones = jnp.ones((WIN, width), jnp.bfloat16)
            values = jnp.concatenate([values, ones], axis=1)
            gathered = jnp.zeros((WIN, width), jnp.float32)
            for head in range(heads):
                own = jnp.where(lane_head == head, queries, jnp.zeros_like(queries))
                scores = lax.dot_general(
                    own, keys, (((1,), (1,)), ((), ())), preferred_element_type=jnp.float32
                ) * HD ** (-0.5)
                at = (window * HEADS + group * 4 + head) * WIN
                scores = scores + jnp.concatenate(
                    [addend_ref[0, at : at + WIN, :], addend_ref[1, at : at + WIN, 0 : WIN - 128]],
                    axis=1,
                )
                raised = jnp.exp(scores - jnp.max(scores, axis=-1, keepdims=True))
                mixed = jnp.dot(
                    raised.astype(jnp.bfloat16), values, preferred_element_type=jnp.float32
                )
                mixed = mixed[:, :width] / mixed[:, width:]
                gathered = jnp.where(lane_head == head, mixed, gathered)
            attended_ref[first : first + WIN, lanes : lanes + width] = gathered.astype(jnp.bfloat16)
    mid = (
        field_ref[...]
        + jnp.dot(attended_ref[...], proj_w[0], preferred_element_type=jnp.float32)
        + out_b[0, 0:1].astype(jnp.float32)
    )
    normed_two = layer_norm(mid, ln_g[0, 1:2], ln_s[0, 1:2]).astype(jnp.bfloat16)
    hidden = jnp.dot(normed_two, fc1_w[0], preferred_element_type=jnp.float32)
    hidden = hidden + fc1_b[...].astype(jnp.float32)
    hidden = (hidden * 0.5 * (1.0 + lax.erf(hidden * np.float32(np.sqrt(0.5))))).astype(
        jnp.bfloat16
    )
    field_ref[...] = (
        mid
        + jnp.dot(hidden, fc2_w[0], preferred_element_type=jnp.float32)
        + out_b[0, 1:2].astype(jnp.float32)
    )


def first_kernel(patch_ref, arrange_ref, *refs):
    params, (addend_ref,), outs = refs[:9], refs[9:10], refs[10:14]
    field_ref, packed_ref, attended_ref, quarter_ref = refs[14:]

    @pl.when(lax.axis_index("section") == 0)
    def work():
        for lat in range(WLAT):
            for lon in range(WLON):
                at = (lat * WLON + lon) * 4
                field_ref[at : at + 4, :] = patch_ref[0, lat, lon].astype(jnp.float32)
        field_ref[...] = jnp.dot(
            arrange_ref[...],
            field_ref[...].astype(jnp.bfloat16),
            preferred_element_type=jnp.float32,
        )
        run_block(field_ref, params, addend_ref, packed_ref, attended_ref)
        for quarter in range(4):
            for place in range(4):
                lev = (place + 1) % 4
                at = (lev // 2) * WIN + quarter * QUARTER + (lev % 2) * PIECE
                quarter_ref[place * PIECE : (place + 1) * PIECE, :] = field_ref[at : at + PIECE, :]
            outs[quarter][...] = quarter_ref[...].astype(jnp.bfloat16)


def second_kernel(*refs):
    quarters, params, (addend_ref,), outs = refs[:4], refs[4:13], refs[13:14], refs[14:18]
    field_ref, packed_ref, attended_ref, quarter_ref = refs[18:]

    @pl.when(lax.axis_index("section") == 1)
    def work():
        for quarter in range(4):
            held = quarters[quarter][...].astype(jnp.float32)
            for window in range(2):
                at = window * WIN + quarter * QUARTER
                field_ref[at : at + QUARTER, :] = held[window * QUARTER : (window + 1) * QUARTER]
        run_block(field_ref, params, addend_ref, packed_ref, attended_ref)
        for quarter in range(4):
            for window in range(2):
                at = window * WIN + quarter * QUARTER
                quarter_ref[window * QUARTER : (window + 1) * QUARTER, :] = field_ref[
                    at : at + QUARTER, :
                ]
            outs[quarter][...] = quarter_ref[...].astype(jnp.bfloat16)


def place_kernel(*refs):
    arrange_ref, out_ref, grid_ref = refs[8:]

    def place(quarters):
        held = jnp.concatenate([quarter[...] for quarter in quarters], axis=0)
        grid_ref[...] = jnp.dot(arrange_ref[...], held, preferred_element_type=jnp.float32)
        for lat in range(WLAT):
            for lon in range(WLON):
                at = (lat * WLON + lon) * 4
                out_ref[0, lat, lon] = grid_ref[at : at + 4, :].astype(jnp.bfloat16)

    section = lax.axis_index("section")
    pl.when(section == 0)(lambda: place(refs[0:4]))
    pl.when(section == 1)(lambda: place(refs[4:8]))


def call(kernel, operands, outs, scratch, flops):
    whole = pl.BlockSpec(memory_space=pltpu.VMEM)
    moved = sum(op.size * op.dtype.itemsize for op in operands)
    return pl.pallas_call(
        kernel,
        out_shape=outs,
        in_specs=[whole] * len(operands),
        out_specs=jax.tree.map(lambda unused: whole, outs),
        scratch_shapes=scratch,
        compiler_params=pltpu.CompilerParams(vmem_limit_bytes=VMEM_LIMIT),
        cost_estimate=pl.CostEstimate(flops=flops, bytes_accessed=moved, transcendentals=0),
    )(*operands)


QUARTERS = [jax.ShapeDtypeStruct((2 * QUARTER, C), jnp.bfloat16)] * 4
BLOCK_SCRATCH = [
    pltpu.VMEM((2 * WIN, C), jnp.float32),
    pltpu.VMEM((2 * WIN, 3 * 384), jnp.bfloat16),
    pltpu.VMEM((2 * WIN, C), jnp.bfloat16),
    pltpu.VMEM((2 * QUARTER, C), jnp.float32),
]
BLOCK_FLOPS = 800_000_000


def send(block, source, target, lat_step, lon_step):
    lons, lats = lax.axis_size("lon"), lax.axis_size("lat")
    route = []
    for lon in range(lons):
        for lat in range(lats):
            there = ((lon + lon_step) % lons) * lats + (lat + lat_step) % lats
            route.append(((lon * lats + lat) * 2 + source, there * 2 + target))
    return lax.ppermute(block, AXES, route)


def to_shifted(quarters):
    moved = [send(quarters[q], 0, 1, q // 2 - 1, q % 2 - 1) for q in range(4)]
    return [moved[3 - q] for q in range(4)]


def body(
    inputs,
    ln_gain,
    ln_shift,
    qkv_weight,
    qkv_bias,
    proj_weight,
    fc1_weight,
    fc1_bias,
    fc2_weight,
    out_bias,
    bias_table,
):
    params = (
        ln_gain,
        ln_shift,
        qkv_weight,
        qkv_bias,
        proj_weight,
        fc1_weight,
        fc1_bias,
        fc2_weight,
        out_bias,
    )
    patch = inputs.transpose(0, 2, 3, 1, 4)
    other = send(patch, 1, 0, 0, 0)
    addend = call(
        prepare_kernel,
        (bias_table, jnp.asarray(spread_matrix())),
        jax.ShapeDtypeStruct((2, 2 * HEADS * WIN, 128), jnp.float32),
        [pltpu.VMEM((32, bias_table.shape[-1]), jnp.float32)],
        200_000_000,
    )
    arrange = jnp.asarray(arrange_matrix())
    block_one = functools.partial(
        call, first_kernel, outs=QUARTERS, scratch=BLOCK_SCRATCH, flops=BLOCK_FLOPS
    )
    block_two = functools.partial(
        call, second_kernel, outs=QUARTERS, scratch=BLOCK_SCRATCH, flops=BLOCK_FLOPS
    )
    own_shifted = to_shifted(block_one((patch, arrange, *params, addend)))
    other_shifted = to_shifted(block_one((other, arrange, *params, addend)))
    own_done = block_two((*own_shifted, *params, addend))
    own_back = [send(own_done[3 - q], 1, 0, 1 - q // 2, 1 - q % 2) for q in range(4)]
    other_done = block_two((*other_shifted, *params, addend))
    other_back = [send(other_done[3 - q], 1, 1, 1 - q // 2, 1 - q % 2) for q in range(3)]
    placed = call(
        place_kernel,
        (*own_back, *other_back, other_done[0], jnp.asarray(place_matrix())),
        jax.ShapeDtypeStruct(patch.shape, patch.dtype),
        [pltpu.VMEM((2 * WIN, C), jnp.float32)],
        1_000_000,
    )
    return placed.transpose(0, 3, 1, 2, 4)


def solution(mesh):
    return jax.shard_map(
        body,
        mesh=mesh,
        in_specs=(
            P("section", None, "lat", "lon", None),
            P("section", None, None),
            P("section", None, None),
            P("section", None, None),
            P("section", None),
            P("section", None, None),
            P("section", None, None),
            P("section", None),
            P("section", None, None),
            P("section", None, None),
            P("section", None, "lat", None, None),
        ),
        out_specs=P("section", None, "lat", "lon", None),
        check_vma=False,
    )
```

```python
import functools

import jax
import jax.numpy as jnp
import numpy as np
from jax import lax
from jax.experimental import pallas as pl
from jax.experimental.pallas import tpu as pltpu
from jax.sharding import PartitionSpec as P

HD = 32
HEADS = 10
C = 320
WLEV = 2
WLAT = 6
WLON = 12
WIN = WLEV * WLAT * WLON
QUARTER = WIN // 4
PIECE = QUARTER // WLEV
SPAN = 2 * WLON - 1
AXES = ("lon", "lat", "section")
VMEM_LIMIT = 20 * 1024 * 1024


def token_row(lev, lat, lon):
    quarter = (lat // 3) * 2 + lon // 6
    return quarter * QUARTER + lev * PIECE + (lat % 3) * 6 + lon % 6


def spread_matrix():
    spread = np.zeros((WLEV * WLAT * SPAN, WLON, 256), np.float32)
    for lev in range(WLEV):
        for lat in range(WLAT):
            for lon in range(WLON):
                for query_lon in range(WLON):
                    source = (lev * WLAT + lat) * SPAN + query_lon - lon + WLON - 1
                    spread[source, query_lon, token_row(lev, lat, lon)] = 1.0
    return spread.reshape(WLEV * WLAT * SPAN, WLON * 256).astype(jnp.bfloat16)


def arrange_matrix():
    arrange = np.zeros((2 * WIN, 2 * WIN), np.float32)
    for lev in range(4):
        for lat in range(WLAT):
            for lon in range(WLON):
                row = (lev // 2) * WIN + token_row(lev % 2, lat, lon)
                arrange[row, (lat * WLON + lon) * 4 + lev] = 1.0
    return arrange.astype(jnp.bfloat16)


def place_matrix():
    arrange = np.zeros((2 * WIN, 2 * WIN), np.float32)
    for lev in range(4):
        for lat in range(WLAT):
            for lon in range(WLON):
                quarter = (lat // 3) * 2 + lon // 6
                source = ((quarter * 4 + (lev + 3) % 4) * 3 + lat % 3) * 6 + lon % 6
                arrange[(lat * WLON + lon) * 4 + lev, source] = 1.0
    return arrange.astype(jnp.bfloat16)


def lay_out_bias(table_ref, spread_ref, addend_ref, wide_ref):
    for head in range(HEADS):
        wide_ref[2 * head : 2 * head + 2, :] = table_ref[0, 0, head].astype(jnp.float32)
    for lev in range(WLEV):
        for lat in range(WLAT):
            parts = []
            for key_lev in range(WLEV):
                for key_lat in range(WLAT):
                    at = ((key_lev * WLEV + lev) * WLAT * WLAT + key_lat * WLAT + lat) * SPAN
                    parts.append(wide_ref[:, at : at + SPAN])
            rows = jnp.concatenate(parts, axis=1).astype(jnp.bfloat16)
            dense = jnp.dot(rows, spread_ref[...], preferred_element_type=jnp.float32)
            for lon in range(WLON):
                row = token_row(lev, lat, lon)
                for tile in range(2):
                    lanes = lon * 256 + tile * 128
                    addend_ref[tile, pl.ds(row, 2 * HEADS, stride=WIN), :] = dense[
                        : 2 * HEADS, lanes : lanes + 128
                    ]


def fetch(sources, targets, sems):
    copies = [
        pltpu.make_async_copy(source, target, sems.at[at])
        for at, (source, target) in enumerate(zip(sources, targets, strict=True))
    ]
    for copy in copies:
        copy.start()
    return copies


def prepare_kernel(table_hbm, spread_hbm, after_ref, addend_ref, table_ref, spread_ref, wide_ref, sems):
    last_lat = lax.axis_index("lat") == lax.axis_size("lat") - 1

    @pl.when(lax.axis_index("section") == 1)
    def work():
        for copy in fetch((table_hbm, spread_hbm), (table_ref, spread_ref), sems):
            copy.wait()
        lay_out_bias(table_ref, spread_ref, addend_ref, wide_ref)
        for tile in range(2):
            query = lax.broadcasted_iota(jnp.int32, (WIN, 128), 0)
            key = lax.broadcasted_iota(jnp.int32, (WIN, 128), 1) + tile * 128
            lat_differs = jnp.logical_and((query >= 2 * QUARTER) != (key >= 2 * QUARTER), last_lat)
            lev_differs = (query % QUARTER >= PIECE) != (key % QUARTER >= PIECE)
            for window in range(2):
                barred = jnp.logical_or(lat_differs, lev_differs) if window else lat_differs
                for head in range(HEADS):
                    at = (2 * head + window) * WIN
                    addend_ref[tile, at : at + WIN, :] = jnp.where(
                        barred, jnp.float32(-1e30), addend_ref[tile, at : at + WIN, :]
                    )


def layer_norm(values, norm_gain, norm_shift):
    center = values - jnp.mean(values, axis=-1, keepdims=True)
    spread = jnp.mean(center * center, axis=-1, keepdims=True)
    return center * lax.rsqrt(spread + 1e-05) * norm_gain.astype(jnp.float32) + norm_shift.astype(
        jnp.float32
    )


def run_block(field_ref, params, copies, addend_ref, packed_ref, attended_ref):
    ln_g, ln_s, qkv_w, qkv_b, proj_w, fc1_w, fc1_b, fc2_w, out_b = params
    for copy in copies[:4]:
        copy.wait()
    normed = layer_norm(field_ref[...], ln_g[0, 0:1], ln_s[0, 0:1]).astype(jnp.bfloat16)
    packed = jnp.dot(normed, qkv_w[0], preferred_element_type=jnp.float32)
    packed = (packed + qkv_b[...].astype(jnp.float32)).astype(jnp.bfloat16)
    packed_ref[:, 0:C] = packed[:, 0:C]
    packed_ref[:, 384 : 384 + C] = packed[:, C : 2 * C]
    packed_ref[:, 768 : 768 + C] = packed[:, 2 * C :]
    for window in range(2):
        first = window * WIN
        for group in range(3):
            width = 128 if group < 2 else 64
            heads = width // HD
            lanes = group * 128
            queries = packed_ref[first : first + WIN, lanes : lanes + width]
            keys = packed_ref[first : first + WIN, 384 + lanes : 384 + lanes + width]
            values = packed_ref[first : first + WIN, 768 + lanes : 768 + lanes + width]
            lane_head = lax.broadcasted_iota(jnp.int32, (WIN, width), 1) // HD
            ones = jnp.ones((WIN, width), jnp.bfloat16)
            values = jnp.concatenate([values, ones], axis=1)
            gathered = jnp.zeros((WIN, width), jnp.float32)
            for head in range(heads):
                own = jnp.where(lane_head == head, queries, jnp.zeros_like(queries))
                scores = lax.dot_general(
                    own, keys, (((1,), (1,)), ((), ())), preferred_element_type=jnp.float32
                ) * HD ** (-0.5)
                at = (2 * (group * 4 + head) + window) * WIN
                scores = scores + jnp.concatenate(
                    [addend_ref[0, at : at + WIN, :], addend_ref[1, at : at + WIN, 0 : WIN - 128]],
                    axis=1,
                )
                raised = jnp.exp(scores - jnp.max(scores, axis=-1, keepdims=True))
                mixed = jnp.dot(
                    raised.astype(jnp.bfloat16), values, preferred_element_type=jnp.float32
                )
                mixed = mixed[:, :width] / mixed[:, width:]
                gathered = jnp.where(lane_head == head, mixed, gathered)
            attended_ref[first : first + WIN, lanes : lanes + width] = gathered.astype(jnp.bfloat16)
    for copy in copies[4:]:
        copy.wait()
    mid = (
        field_ref[...]
        + jnp.dot(attended_ref[...], proj_w[0], preferred_element_type=jnp.float32)
        + out_b[0, 0:1].astype(jnp.float32)
    )
    normed_two = layer_norm(mid, ln_g[0, 1:2], ln_s[0, 1:2]).astype(jnp.bfloat16)
    hidden = jnp.dot(normed_two, fc1_w[0], preferred_element_type=jnp.float32)
    hidden = hidden + fc1_b[...].astype(jnp.float32)
    hidden = (hidden * 0.5 * (1.0 + lax.erf(hidden * np.float32(np.sqrt(0.5))))).astype(
        jnp.bfloat16
    )
    field_ref[...] = (
        mid
        + lax.dot_general(
            hidden, fc2_w[0], (((1,), (1,)), ((), ())), preferred_element_type=jnp.float32
        )
        + out_b[0, 1:2].astype(jnp.float32)
    )


def first_kernel(prepares, patch_ref, arrange_hbm, *refs):
    hbm, refs = refs[:9], refs[9:]
    if prepares:
        table_hbm, spread_hbm = refs[:2]
        outs, addend_ref, refs = refs[2:6], refs[6], refs[7:]
    else:
        addend_ref, outs, refs = refs[0], refs[1:5], refs[5:]
    field_ref, packed_ref, attended_ref, quarter_ref, arrange_ref = refs[:5]
    params, sems = refs[5:14], refs[14]

    @pl.when(lax.axis_index("section") == 0)
    def work():
        if prepares:
            own_ref, table_ref, spread_ref, wide_ref, more_sems = refs[15:]
            early = fetch(
                (table_hbm, spread_hbm, patch_ref), (table_ref, spread_ref, own_ref), more_sems
            )
        else:
            own_ref = patch_ref
        (arranging,) = fetch((arrange_hbm,), (arrange_ref,), sems.at[pl.ds(9, 1)])
        copies = fetch(hbm, params, sems)
        if prepares:
            for copy in early:
                copy.wait()
            lay_out_bias(table_ref, spread_ref, addend_ref, wide_ref)
        for lat in range(WLAT):
            for lon in range(WLON):
                at = (lat * WLON + lon) * 4
                field_ref[at : at + 4, :] = own_ref[0, lat, lon].astype(jnp.float32)
        arranging.wait()
        field_ref[...] = jnp.dot(
            arrange_ref[...],
            field_ref[...].astype(jnp.bfloat16),
            preferred_element_type=jnp.float32,
        )
        run_block(field_ref, params, copies, addend_ref, packed_ref, attended_ref)
        for quarter in range(4):
            for place in range(4):
                lev = (place + 1) % 4
                at = (lev // 2) * WIN + quarter * QUARTER + (lev % 2) * PIECE
                quarter_ref[place * PIECE : (place + 1) * PIECE, :] = field_ref[at : at + PIECE, :]
            outs[quarter][...] = quarter_ref[...].astype(jnp.bfloat16)


def second_kernel(*refs):
    quarters, hbm, (addend_ref,), outs = refs[:4], refs[4:13], refs[13:14], refs[14:18]
    field_ref, packed_ref, attended_ref, quarter_ref = refs[18:22]
    params, sems = refs[22:31], refs[31]

    @pl.when(lax.axis_index("section") == 1)
    def work():
        copies = fetch(hbm, params, sems)
        for quarter in range(4):
            held = quarters[quarter][...].astype(jnp.float32)
            for window in range(2):
                at = window * WIN + quarter * QUARTER
                field_ref[at : at + QUARTER, :] = held[window * QUARTER : (window + 1) * QUARTER]
        run_block(field_ref, params, copies, addend_ref, packed_ref, attended_ref)
        for quarter in range(4):
            for window in range(2):
                at = window * WIN + quarter * QUARTER
                quarter_ref[window * QUARTER : (window + 1) * QUARTER, :] = field_ref[
                    at : at + QUARTER, :
                ]
            outs[quarter][...] = quarter_ref[...].astype(jnp.bfloat16)


def place_kernel(*refs):
    arrange_ref, out_ref, grid_ref = refs[8:]

    def place(quarters):
        held = jnp.concatenate([quarter[...] for quarter in quarters], axis=0)
        grid_ref[...] = jnp.dot(arrange_ref[...], held, preferred_element_type=jnp.float32)
        for lat in range(WLAT):
            for lon in range(WLON):
                at = (lat * WLON + lon) * 4
                out_ref[0, lat, lon] = grid_ref[at : at + 4, :].astype(jnp.bfloat16)

    section = lax.axis_index("section")
    pl.when(section == 0)(lambda: place(refs[0:4]))
    pl.when(section == 1)(lambda: place(refs[4:8]))


def call(kernel, operands, places, outs, scratch, flops):
    spaces = {"h": pltpu.HBM, "v": pltpu.VMEM}
    operands = [
        pltpu.with_memory_space_constraint(operand, pltpu.HBM) if place == "h" else operand
        for operand, place in zip(operands, places, strict=True)
    ]
    return pl.pallas_call(
        kernel,
        out_shape=outs,
        in_specs=[pl.BlockSpec(memory_space=spaces[place]) for place in places],
        out_specs=jax.tree.map(lambda unused: pl.BlockSpec(memory_space=pltpu.VMEM), outs),
        scratch_shapes=scratch,
        compiler_params=pltpu.CompilerParams(vmem_limit_bytes=VMEM_LIMIT),
        cost_estimate=pl.CostEstimate(flops=flops, bytes_accessed=4_000_000, transcendentals=0),
    )(*operands)


QUARTERS = [jax.ShapeDtypeStruct((2 * QUARTER, C), jnp.bfloat16)] * 4
BLOCK_SCRATCH = [
    pltpu.VMEM((2 * WIN, C), jnp.float32),
    pltpu.VMEM((2 * WIN, 3 * 384), jnp.bfloat16),
    pltpu.VMEM((2 * WIN, C), jnp.bfloat16),
    pltpu.VMEM((2 * QUARTER, C), jnp.float32),
]
BLOCK_FLOPS = 800_000_000


def held(array):
    return pltpu.VMEM(array.shape, array.dtype)


def mirrored(lon):
    lons = lax.axis_size("lon")
    across = 4 if lons % 4 == 0 else 1
    return (lons // across - 1 - lon // across) * across + lon % across


def straight(lon):
    return lon


def send(block, sections, steps, source_at, target_at):
    lons, lats = lax.axis_size("lon"), lax.axis_size("lat")
    route = []
    for lon in range(lons):
        for lat in range(lats):
            here = source_at(lon) * lats + lat
            there = target_at((lon + steps[1]) % lons) * lats + (lat + steps[0]) % lats
            route.append((here * 2 + sections[0], there * 2 + sections[1]))
    return lax.ppermute(block, AXES, route)


def to_shifted(quarters, source_at, target_at):
    moved = [
        send(quarters[q], (0, 1), (q // 2 - 1, q % 2 - 1), source_at, target_at) for q in range(4)
    ]
    return [moved[3 - q] for q in range(4)]


def body(
    inputs,
    ln_gain,
    ln_shift,
    qkv_weight,
    qkv_bias,
    proj_weight,
    fc1_weight,
    fc1_bias,
    fc2_weight,
    out_bias,
    bias_table,
):
    params = (
        ln_gain,
        ln_shift,
        qkv_weight,
        qkv_bias,
        proj_weight,
        fc1_weight,
        fc1_bias,
        fc2_weight,
        out_bias,
    )
    params = (*params[:7], fc2_weight.transpose(0, 2, 1), out_bias)
    patch = inputs.transpose(0, 2, 3, 1, 4)
    table = bias_table.transpose(0, 2, 3, 1, 4)
    other = send(patch, (1, 0), (0, 0), straight, mirrored)
    arrange = jnp.asarray(arrange_matrix())
    spread = jnp.asarray(spread_matrix())
    addend_shape = jax.ShapeDtypeStruct((2, 2 * HEADS * WIN, 128), jnp.float32)
    wide = pltpu.VMEM((24, table.shape[-1]), jnp.float32)
    first_scratch = [
        *BLOCK_SCRATCH,
        held(arrange),
        *map(held, params),
        pltpu.SemaphoreType.DMA((10,)),
    ]
    second_scratch = [*BLOCK_SCRATCH, *map(held, params), pltpu.SemaphoreType.DMA((9,))]
    *own_first, addend_one = call(
        functools.partial(first_kernel, True),
        (patch, arrange, *params, table, spread),
        "h" * 13,
        [*QUARTERS, addend_shape],
        [
            *first_scratch,
            held(patch),
            held(table),
            held(spread),
            wide,
            pltpu.SemaphoreType.DMA((3,)),
        ],
        BLOCK_FLOPS,
    )
    own_shifted = to_shifted(own_first, straight, mirrored)
    addend_two = call(
        prepare_kernel,
        (table, spread, own_first[0]),
        "hhv",
        addend_shape,
        [held(table), held(spread), wide, pltpu.SemaphoreType.DMA((2,))],
        200_000_000,
    )
    other_first = call(
        functools.partial(first_kernel, False),
        (other, arrange, *params, addend_one),
        "vh" + "h" * 9 + "v",
        QUARTERS,
        first_scratch,
        BLOCK_FLOPS,
    )
    other_shifted = to_shifted(other_first, mirrored, straight)
    block_two = functools.partial(
        call,
        second_kernel,
        places="vvvv" + "h" * 9 + "v",
        outs=QUARTERS,
        scratch=second_scratch,
        flops=BLOCK_FLOPS,
    )
    own_done = block_two((*own_shifted, *params, addend_two))
    own_back = [
        send(own_done[3 - q], (1, 0), (1 - q // 2, 1 - q % 2), mirrored, straight)
        for q in range(4)
    ]
    other_done = block_two((*other_shifted, *params, addend_two))
    other_back = [
        send(other_done[3 - q], (1, 1), (1 - q // 2, 1 - q % 2), straight, straight)
        for q in range(3)
    ]
    placed = call(
        place_kernel,
        (*own_back, *other_back, other_done[0], jnp.asarray(place_matrix())),
        "v" * 9,
        jax.ShapeDtypeStruct(patch.shape, patch.dtype),
        [pltpu.VMEM((2 * WIN, C), jnp.float32)],
        1_000_000,
    )
    return placed.transpose(0, 3, 1, 2, 4)


def solution(mesh):
    return jax.shard_map(
        body,
        mesh=mesh,
        in_specs=(
            P("section", None, "lat", "lon", None),
            P("section", None, None),
            P("section", None, None),
            P("section", None, None),
            P("section", None),
            P("section", None, None),
            P("section", None, None),
            P("section", None),
            P("section", None, None),
            P("section", None, None),
            P("section", None, "lat", None, None),
        ),
        out_specs=P("section", None, "lat", "lon", None),
        check_vma=False,
    )
```

```python
import functools

import jax
import jax.numpy as jnp
import numpy as np
from jax import lax
from jax.experimental import pallas as pl
from jax.experimental.pallas import tpu as pltpu
from jax.sharding import PartitionSpec as P

HD = 32
HEADS = 10
C = 320
WLEV = 2
WLAT = 6
WLON = 12
WIN = WLEV * WLAT * WLON
QUARTER = WIN // 4
PIECE = QUARTER // WLEV
SPAN = 2 * WLON - 1
AXES = ("lon", "lat", "section")
VMEM_LIMIT = 20 * 1024 * 1024


def token_row(lev, lat, lon):
    quarter = (lat // 3) * 2 + lon // 6
    return quarter * QUARTER + lev * PIECE + (lat % 3) * 6 + lon % 6


def spread_matrix():
    spread = np.zeros((WLEV * WLAT * SPAN, WLON, 256), np.float32)
    for lev in range(WLEV):
        for lat in range(WLAT):
            for lon in range(WLON):
                for query_lon in range(WLON):
                    source = (lev * WLAT + lat) * SPAN + query_lon - lon + WLON - 1
                    spread[source, query_lon, token_row(lev, lat, lon)] = 1.0
    return spread.reshape(WLEV * WLAT * SPAN, WLON * 256).astype(jnp.bfloat16)


def arrange_matrix():
    arrange = np.zeros((2 * WIN, 2 * WIN), np.float32)
    for lev in range(4):
        for lat in range(WLAT):
            for lon in range(WLON):
                row = (lev // 2) * WIN + token_row(lev % 2, lat, lon)
                arrange[row, (lat * WLON + lon) * 4 + lev] = 1.0
    return arrange.astype(jnp.bfloat16)


def place_matrix():
    arrange = np.zeros((2 * WIN, 2 * WIN), np.float32)
    for lev in range(4):
        for lat in range(WLAT):
            for lon in range(WLON):
                quarter = (lat // 3) * 2 + lon // 6
                source = ((quarter * 4 + (lev + 3) % 4) * 3 + lat % 3) * 6 + lon % 6
                arrange[(lat * WLON + lon) * 4 + lev, source] = 1.0
    return arrange.astype(jnp.bfloat16)


def lay_out_bias(table_ref, spread_ref, addend_ref, wide_ref, rows_ref):
    for head in range(HEADS):
        wide_ref[2 * head : 2 * head + 2, :] = table_ref[0, 0, head].astype(jnp.float32)
    for lev in range(WLEV):
        for lat in range(WLAT):
            parts = []
            for key_lev in range(WLEV):
                for key_lat in range(WLAT):
                    at = ((key_lev * WLEV + lev) * WLAT * WLAT + key_lat * WLAT + lat) * SPAN
                    parts.append(wide_ref[:, at : at + SPAN])
            first = (lev * WLAT + lat) * 24
            rows_ref[first : first + 24, :] = jnp.concatenate(parts, axis=1)
    rows = rows_ref[...].astype(jnp.bfloat16)
    for lon in range(WLON):
        dense = jnp.dot(
            rows, spread_ref[:, lon * 256 : lon * 256 + 256], preferred_element_type=jnp.float32
        )
        for lev in range(WLEV):
            for lat in range(WLAT):
                first = (lev * WLAT + lat) * 24
                row = token_row(lev, lat, lon)
                for tile in range(2):
                    addend_ref[tile, pl.ds(row, 2 * HEADS, stride=WIN), :] = dense[
                        first : first + 2 * HEADS, tile * 128 : tile * 128 + 128
                    ]


def fetch(sources, targets, sems):
    copies = [
        pltpu.make_async_copy(source, target, sems.at[at])
        for at, (source, target) in enumerate(zip(sources, targets, strict=True))
    ]
    for copy in copies:
        copy.start()
    return copies


def pack(quarter_ref):
    rest = jnp.concatenate(
        [quarter_ref[0:QUARTER, 256:C], quarter_ref[QUARTER : 2 * QUARTER, 256:C]], axis=1
    )
    return jnp.concatenate(
        [quarter_ref[:, 0:128], quarter_ref[:, 128:256], rest], axis=0
    ).astype(jnp.bfloat16)


def unpack(packed_ref, target_ref, starts):
    packed = packed_ref[...].astype(jnp.float32)
    for half, at in enumerate(starts):
        rows = slice(at, at + QUARTER)
        target_ref[rows, 0:128] = packed[half * QUARTER : (half + 1) * QUARTER]
        target_ref[rows, 128:256] = packed[(2 + half) * QUARTER : (3 + half) * QUARTER]
        target_ref[rows, 256:C] = packed[4 * QUARTER :, half * 64 : half * 64 + 64]


def prepare_kernel(*refs):
    table_hbm, spread_hbm, hbm = refs[0], refs[1], refs[2:11]
    addend_ref, params = refs[12], refs[13:22]
    table_ref, spread_ref, wide_ref, rows_ref, sems = refs[22:]
    last_lat = lax.axis_index("lat") == lax.axis_size("lat") - 1

    @pl.when(lax.axis_index("section") == 1)
    def work():
        copies = fetch(
            (table_hbm, spread_hbm, *hbm), (table_ref, spread_ref, *params), sems
        )
        for copy in copies:
            copy.wait()
        lay_out_bias(table_ref, spread_ref, addend_ref, wide_ref, rows_ref)
        for tile in range(2):
            query = lax.broadcasted_iota(jnp.int32, (WIN, 128), 0)
            key = lax.broadcasted_iota(jnp.int32, (WIN, 128), 1) + tile * 128
            lat_differs = jnp.logical_and((query >= 2 * QUARTER) != (key >= 2 * QUARTER), last_lat)
            lev_differs = (query % QUARTER >= PIECE) != (key % QUARTER >= PIECE)
            for window in range(2):
                barred = jnp.logical_or(lat_differs, lev_differs) if window else lat_differs
                for head in range(HEADS):
                    at = (2 * head + window) * WIN
                    addend_ref[tile, at : at + WIN, :] = jnp.where(
                        barred, jnp.float32(-1e30), addend_ref[tile, at : at + WIN, :]
                    )


def layer_norm(values, norm_gain, norm_shift):
    center = values - jnp.mean(values, axis=-1, keepdims=True)
    spread = jnp.mean(center * center, axis=-1, keepdims=True)
    return center * lax.rsqrt(spread + 1e-05) * norm_gain.astype(jnp.float32) + norm_shift.astype(
        jnp.float32
    )


def run_block(field_ref, params, copies, addend_ref, packed_ref, attended_ref):
    ln_g, ln_s, qkv_w, qkv_b, proj_w, fc1_w, fc1_b, fc2_w, out_b = params
    for copy in copies[:4]:
        copy.wait()
    normed = layer_norm(field_ref[...], ln_g[0, 0:1], ln_s[0, 0:1]).astype(jnp.bfloat16)
    packed = jnp.dot(normed, qkv_w[0], preferred_element_type=jnp.float32)
    packed = (packed + qkv_b[...].astype(jnp.float32)).astype(jnp.bfloat16)
    packed_ref[:, 0:C] = packed[:, 0:C]
    packed_ref[:, 384 : 384 + C] = packed[:, C : 2 * C]
    packed_ref[:, 768 : 768 + C] = packed[:, 2 * C :]
    for window in range(2):
        first = window * WIN
        for group in range(3):
            width = 128 if group < 2 else 64
            heads = width // HD
            lanes = group * 128
            queries = packed_ref[first : first + WIN, lanes : lanes + width]
            keys = packed_ref[first : first + WIN, 384 + lanes : 384 + lanes + width]
            values = packed_ref[first : first + WIN, 768 + lanes : 768 + lanes + width]
            lane_head = lax.broadcasted_iota(jnp.int32, (WIN, width), 1) // HD
            ones = jnp.ones((WIN, width), jnp.bfloat16)
            values = jnp.concatenate([values, ones], axis=1)
            gathered = jnp.zeros((WIN, width), jnp.float32)
            for head in range(heads):
                own = jnp.where(lane_head == head, queries, jnp.zeros_like(queries))
                scores = lax.dot_general(
                    own, keys, (((1,), (1,)), ((), ())), preferred_element_type=jnp.float32
                ) * HD ** (-0.5)
                at = (2 * (group * 4 + head) + window) * WIN
                scores = scores + jnp.concatenate(
                    [addend_ref[0, at : at + WIN, :], addend_ref[1, at : at + WIN, 0 : WIN - 128]],
                    axis=1,
                )
                raised = jnp.exp(scores - jnp.max(scores, axis=-1, keepdims=True))
                mixed = jnp.dot(
                    raised.astype(jnp.bfloat16), values, preferred_element_type=jnp.float32
                )
                mixed = mixed[:, :width] / mixed[:, width:]
                gathered = jnp.where(lane_head == head, mixed, gathered)
            attended_ref[first : first + WIN, lanes : lanes + width] = gathered.astype(jnp.bfloat16)
    for copy in copies[4:]:
        copy.wait()
    mid = (
        field_ref[...]
        + jnp.dot(attended_ref[...], proj_w[0], preferred_element_type=jnp.float32)
        + out_b[0, 0:1].astype(jnp.float32)
    )
    normed_two = layer_norm(mid, ln_g[0, 1:2], ln_s[0, 1:2]).astype(jnp.bfloat16)
    hidden = jnp.dot(normed_two, fc1_w[0], preferred_element_type=jnp.float32)
    hidden = hidden + fc1_b[...].astype(jnp.float32)
    hidden = (hidden * 0.5 * (1.0 + lax.erf(hidden * np.float32(np.sqrt(0.5))))).astype(
        jnp.bfloat16
    )
    field_ref[...] = (
        mid
        + lax.dot_general(
            hidden, fc2_w[0], (((1,), (1,)), ((), ())), preferred_element_type=jnp.float32
        )
        + out_b[0, 1:2].astype(jnp.float32)
    )


def first_kernel(prepares, *refs):
    if prepares:
        patch_hbm, arrange_hbm, hbm, table_hbm, spread_hbm = *refs[:2], refs[2:11], *refs[11:13]
        outs, addend_ref, arrange_ref, params = refs[13:17], refs[17], refs[18], refs[19:28]
        field_ref, packed_ref, attended_ref, quarter_ref = refs[28:32]
        patch_ref, table_ref, spread_ref, wide_ref, rows_ref, sems = refs[32:]
    else:
        patch_ref, arrange_ref, params, addend_ref = *refs[:2], refs[2:11], refs[11]
        outs, (field_ref, packed_ref, attended_ref, quarter_ref) = refs[12:16], refs[16:]

    @pl.when(lax.axis_index("section") == 0)
    def work():
        copies = []
        if prepares:
            copies = fetch(
                (table_hbm, spread_hbm, patch_hbm, arrange_hbm, *hbm),
                (table_ref, spread_ref, patch_ref, arrange_ref, *params),
                sems,
            )
            for copy in copies[:4]:
                copy.wait()
            copies = copies[4:]
            lay_out_bias(table_ref, spread_ref, addend_ref, wide_ref, rows_ref)
        for lat in range(WLAT):
            for lon in range(WLON):
                at = (lat * WLON + lon) * 4
                field_ref[at : at + 4, :] = patch_ref[0, lat, lon].astype(jnp.float32)
        field_ref[...] = jnp.dot(
            arrange_ref[...],
            field_ref[...].astype(jnp.bfloat16),
            preferred_element_type=jnp.float32,
        )
        run_block(field_ref, params, copies, addend_ref, packed_ref, attended_ref)
        for quarter in range(4):
            for place in range(4):
                lev = (place + 1) % 4
                at = (lev // 2) * WIN + quarter * QUARTER + (lev % 2) * PIECE
                quarter_ref[place * PIECE : (place + 1) * PIECE, :] = field_ref[at : at + PIECE, :]
            outs[quarter][...] = pack(quarter_ref)


def second_kernel(*refs):
    quarters, params, addend_ref, outs = refs[:4], refs[4:13], refs[13], refs[14:18]
    field_ref, packed_ref, attended_ref, quarter_ref = refs[18:]

    @pl.when(lax.axis_index("section") == 1)
    def work():
        for quarter in range(4):
            at = quarter * QUARTER
            unpack(quarters[quarter], field_ref, (at, WIN + at))
        run_block(field_ref, params, [], addend_ref, packed_ref, attended_ref)
        for quarter in range(4):
            for window in range(2):
                at = window * WIN + quarter * QUARTER
                quarter_ref[window * QUARTER : (window + 1) * QUARTER, :] = field_ref[
                    at : at + QUARTER, :
                ]
            outs[quarter][...] = pack(quarter_ref)


def place_kernel(*refs):
    arrange_ref, out_ref, grid_ref = refs[8:]

    def place(quarters):
        for at, quarter in enumerate(quarters):
            unpack(quarter, grid_ref, (2 * at * QUARTER, (2 * at + 1) * QUARTER))
        grid_ref[...] = jnp.dot(
            arrange_ref[...],
            grid_ref[...].astype(jnp.bfloat16),
            preferred_element_type=jnp.float32,
        )
        for lat in range(WLAT):
            for lon in range(WLON):
                at = (lat * WLON + lon) * 4
                out_ref[0, lat, lon] = grid_ref[at : at + 4, :].astype(jnp.bfloat16)

    section = lax.axis_index("section")
    pl.when(section == 0)(lambda: place(refs[0:4]))
    pl.when(section == 1)(lambda: place(refs[4:8]))


def call(kernel, operands, places, outs, scratch, flops):
    spaces = {"h": pltpu.HBM, "v": pltpu.VMEM}
    operands = [
        pltpu.with_memory_space_constraint(operand, pltpu.HBM) if place == "h" else operand
        for operand, place in zip(operands, places, strict=True)
    ]
    return pl.pallas_call(
        kernel,
        out_shape=outs,
        in_specs=[pl.BlockSpec(memory_space=spaces[place]) for place in places],
        out_specs=jax.tree.map(lambda unused: pl.BlockSpec(memory_space=pltpu.VMEM), outs),
        scratch_shapes=scratch,
        compiler_params=pltpu.CompilerParams(vmem_limit_bytes=VMEM_LIMIT),
        cost_estimate=pl.CostEstimate(flops=flops, bytes_accessed=4_000_000, transcendentals=0),
    )(*operands)


QUARTERS = [jax.ShapeDtypeStruct((5 * QUARTER, 128), jnp.bfloat16)] * 4
BLOCK_SCRATCH = [
    pltpu.VMEM((2 * WIN, C), jnp.float32),
    pltpu.VMEM((2 * WIN, 3 * 384), jnp.bfloat16),
    pltpu.VMEM((2 * WIN, C), jnp.bfloat16),
    pltpu.VMEM((2 * QUARTER, C), jnp.float32),
]
BLOCK_FLOPS = 800_000_000


def held(array):
    return pltpu.VMEM(array.shape, array.dtype)


def mirrored(lon):
    lons = lax.axis_size("lon")
    across = 4 if lons % 4 == 0 else 1
    return (lons // across - 1 - lon // across) * across + lon % across


def straight(lon):
    return lon


def send(block, sections, steps, source_at, target_at):
    lons, lats = lax.axis_size("lon"), lax.axis_size("lat")
    route = []
    for lon in range(lons):
        for lat in range(lats):
            here = source_at(lon) * lats + lat
            there = target_at((lon + steps[1]) % lons) * lats + (lat + steps[0]) % lats
            route.append((here * 2 + sections[0], there * 2 + sections[1]))
    return lax.ppermute(block, AXES, route)


def to_shifted(quarters, source_at, target_at):
    moved = [
        send(quarters[q], (0, 1), (q // 2 - 1, q % 2 - 1), source_at, target_at) for q in range(4)
    ]
    return [moved[3 - q] for q in range(4)]


def body(
    inputs,
    ln_gain,
    ln_shift,
    qkv_weight,
    qkv_bias,
    proj_weight,
    fc1_weight,
    fc1_bias,
    fc2_weight,
    out_bias,
    bias_table,
):
    params = (
        ln_gain,
        ln_shift,
        qkv_weight,
        qkv_bias,
        proj_weight,
        fc1_weight,
        fc1_bias,
        fc2_weight,
        out_bias,
    )
    params = (*params[:7], fc2_weight.transpose(0, 2, 1), out_bias)
    patch = inputs.transpose(0, 2, 3, 1, 4)
    table = bias_table.transpose(0, 2, 3, 1, 4)
    other = send(patch, (1, 0), (0, 0), straight, mirrored)
    arrange = jnp.asarray(arrange_matrix())
    spread = jnp.asarray(spread_matrix())
    addend_shape = jax.ShapeDtypeStruct((2, 2 * HEADS * WIN, 128), jnp.float32)
    bias_scratch = [
        held(table),
        held(spread),
        pltpu.VMEM((24, table.shape[-1]), jnp.float32),
        pltpu.VMEM((12 * 24, spread.shape[0]), jnp.float32),
    ]
    brought = [jax.ShapeDtypeStruct(member.shape, member.dtype) for member in params]
    made = call(
        functools.partial(first_kernel, True),
        (patch, arrange, *params, table, spread),
        "h" * 13,
        [*QUARTERS, addend_shape, jax.ShapeDtypeStruct(arrange.shape, arrange.dtype), *brought],
        [*BLOCK_SCRATCH, held(patch), *bias_scratch, pltpu.SemaphoreType.DMA((13,))],
        BLOCK_FLOPS,
    )
    own_first, (addend_one, arranging), params_one = made[:4], made[4:6], made[6:]
    own_shifted = to_shifted(own_first, straight, mirrored)
    addend_two, *params_two = call(
        prepare_kernel,
        (table, spread, *params, own_first[0]),
        "h" * 11 + "v",
        [addend_shape, *brought],
        [*bias_scratch, pltpu.SemaphoreType.DMA((11,))],
        200_000_000,
    )
    other_first = call(
        functools.partial(first_kernel, False),
        (other, arranging, *params_one, addend_one),
        "v" * 12,
        QUARTERS,
        BLOCK_SCRATCH,
        BLOCK_FLOPS,
    )
    other_shifted = to_shifted(other_first, mirrored, straight)
    block_two = functools.partial(
        call,
        second_kernel,
        places="v" * 14,
        outs=QUARTERS,
        scratch=BLOCK_SCRATCH,
        flops=BLOCK_FLOPS,
    )
    own_done = block_two((*own_shifted, *params_two, addend_two))
    own_back = [
        send(own_done[3 - q], (1, 0), (1 - q // 2, 1 - q % 2), mirrored, straight)
        for q in range(4)
    ]
    other_done = block_two((*other_shifted, *params_two, addend_two))
    across, along, upward = [
        send(other_done[3 - q], (1, 1), (1 - q // 2, 1 - q % 2), straight, straight)
        for q in (0, 2, 1)
    ]
    other_back = (across, upward, along)
    placed = call(
        place_kernel,
        (*own_back, *other_back, other_done[0], jnp.asarray(place_matrix())),
        "v" * 9,
        jax.ShapeDtypeStruct(patch.shape, patch.dtype),
        [pltpu.VMEM((2 * WIN, C), jnp.float32)],
        1_000_000,
    )
    return placed.transpose(0, 3, 1, 2, 4)


def solution(mesh):
    return jax.shard_map(
        body,
        mesh=mesh,
        in_specs=(
            P("section", None, "lat", "lon", None),
            P("section", None, None),
            P("section", None, None),
            P("section", None, None),
            P("section", None),
            P("section", None, None),
            P("section", None, None),
            P("section", None),
            P("section", None, None),
            P("section", None, None),
            P("section", None, "lat", None, None),
        ),
        out_specs=P("section", None, "lat", "lon", None),
        check_vma=False,
    )
```

```python
import functools

import jax
import jax.numpy as jnp
import numpy as np
from jax import lax
from jax.experimental import pallas as pl
from jax.experimental.pallas import tpu as pltpu
from jax.sharding import PartitionSpec as P

HD = 32
HEADS = 10
C = 320
WLEV = 2
WLAT = 6
WLON = 12
WIN = WLEV * WLAT * WLON
QUARTER = WIN // 4
PIECE = QUARTER // WLEV
SPAN = 2 * WLON - 1
AXES = ("lon", "lat", "section")
VMEM_LIMIT = 20 * 1024 * 1024


def token_row(lev, lat, lon):
    quarter = (lat // 3) * 2 + lon // 6
    return quarter * QUARTER + lev * PIECE + (lat % 3) * 6 + lon % 6


def spread_matrix():
    spread = np.zeros((WLEV * WLAT * SPAN, WLON, 256), np.float32)
    for lev in range(WLEV):
        for lat in range(WLAT):
            for lon in range(WLON):
                for query_lon in range(WLON):
                    source = (lev * WLAT + lat) * SPAN + query_lon - lon + WLON - 1
                    spread[source, query_lon, token_row(lev, lat, lon)] = 1.0
    return spread.reshape(WLEV * WLAT * SPAN, WLON * 256).astype(jnp.bfloat16)


def arrange_matrix():
    arrange = np.zeros((2 * WIN, 2 * WIN), np.float32)
    for lev in range(4):
        for lat in range(WLAT):
            for lon in range(WLON):
                row = (lev // 2) * WIN + token_row(lev % 2, lat, lon)
                arrange[row, (lat * WLON + lon) * 4 + lev] = 1.0
    return arrange.astype(jnp.bfloat16)


def place_matrix():
    arrange = np.zeros((2 * WIN, 2 * WIN), np.float32)
    for lev in range(4):
        for lat in range(WLAT):
            for lon in range(WLON):
                quarter = (lat // 3) * 2 + lon // 6
                source = ((quarter * 4 + (lev + 3) % 4) * 3 + lat % 3) * 6 + lon % 6
                arrange[(lat * WLON + lon) * 4 + lev, source] = 1.0
    return arrange.astype(jnp.bfloat16)


def lay_out_bias(table_ref, spread_ref, addend_ref, wide_ref, rows_ref):
    for head in range(HEADS):
        wide_ref[2 * head : 2 * head + 2, :] = table_ref[0, 0, head].astype(jnp.float32)
    for lev in range(WLEV):
        for lat in range(WLAT):
            parts = []
            for key_lev in range(WLEV):
                for key_lat in range(WLAT):
                    at = ((key_lev * WLEV + lev) * WLAT * WLAT + key_lat * WLAT + lat) * SPAN
                    parts.append(wide_ref[:, at : at + SPAN])
            first = (lev * WLAT + lat) * 24
            rows_ref[first : first + 24, :] = jnp.concatenate(parts, axis=1)
    rows = rows_ref[...].astype(jnp.bfloat16)
    for lon in range(WLON):
        dense = jnp.dot(
            rows, spread_ref[:, lon * 256 : lon * 256 + 256], preferred_element_type=jnp.float32
        )
        for lev in range(WLEV):
            for lat in range(WLAT):
                first = (lev * WLAT + lat) * 24
                row = token_row(lev, lat, lon)
                for tile in range(2):
                    addend_ref[tile, pl.ds(row, 2 * HEADS, stride=WIN), :] = dense[
                        first : first + 2 * HEADS, tile * 128 : tile * 128 + 128
                    ]


def fetch(sources, targets, sems):
    copies = [
        pltpu.make_async_copy(source, target, sems.at[at])
        for at, (source, target) in enumerate(zip(sources, targets, strict=True))
    ]
    for copy in copies:
        copy.start()
    return copies


def pack(quarter_ref):
    rest = jnp.concatenate(
        [quarter_ref[0:QUARTER, 256:C], quarter_ref[QUARTER : 2 * QUARTER, 256:C]], axis=1
    )
    return jnp.concatenate(
        [quarter_ref[:, 0:128], quarter_ref[:, 128:256], rest], axis=0
    ).astype(jnp.bfloat16)


def unpack(packed_ref, target_ref, starts):
    packed = packed_ref[...].astype(jnp.float32)
    for half, at in enumerate(starts):
        rows = slice(at, at + QUARTER)
        target_ref[rows, 0:128] = packed[half * QUARTER : (half + 1) * QUARTER]
        target_ref[rows, 128:256] = packed[(2 + half) * QUARTER : (3 + half) * QUARTER]
        target_ref[rows, 256:C] = packed[4 * QUARTER :, half * 64 : half * 64 + 64]


def prepare_kernel(*refs):
    table_hbm, spread_hbm, hbm = refs[0], refs[1], refs[2:11]
    addend_ref, params = refs[12], refs[13:22]
    table_ref, spread_ref, wide_ref, rows_ref, sems = refs[22:]
    last_lat = lax.axis_index("lat") == lax.axis_size("lat") - 1

    @pl.when(lax.axis_index("section") == 1)
    def work():
        copies = fetch(
            (table_hbm, spread_hbm, *hbm), (table_ref, spread_ref, *params), sems
        )
        for copy in copies:
            copy.wait()
        lay_out_bias(table_ref, spread_ref, addend_ref, wide_ref, rows_ref)
        for tile in range(2):
            query = lax.broadcasted_iota(jnp.int32, (WIN, 128), 0)
            key = lax.broadcasted_iota(jnp.int32, (WIN, 128), 1) + tile * 128
            lat_differs = jnp.logical_and((query >= 2 * QUARTER) != (key >= 2 * QUARTER), last_lat)
            lev_differs = (query % QUARTER >= PIECE) != (key % QUARTER >= PIECE)
            for window in range(2):
                barred = jnp.logical_or(lat_differs, lev_differs) if window else lat_differs
                for head in range(HEADS):
                    at = (2 * head + window) * WIN
                    addend_ref[tile, at : at + WIN, :] = jnp.where(
                        barred, jnp.float32(-1e30), addend_ref[tile, at : at + WIN, :]
                    )


def layer_norm(values, norm_gain, norm_shift):
    center = values - jnp.mean(values, axis=-1, keepdims=True)
    spread = jnp.mean(center * center, axis=-1, keepdims=True)
    return center * lax.rsqrt(spread + 1e-05) * norm_gain.astype(jnp.float32) + norm_shift.astype(
        jnp.float32
    )


def run_block(field_ref, params, copies, addend_ref, packed_ref, attended_ref):
    ln_g, ln_s, qkv_w, qkv_b, proj_w, fc1_w, fc1_b, fc2_w, out_b = params
    for copy in copies[:4]:
        copy.wait()
    normed = layer_norm(field_ref[...], ln_g[0, 0:1], ln_s[0, 0:1]).astype(jnp.bfloat16)
    packed = jnp.dot(normed, qkv_w[0], preferred_element_type=jnp.float32)
    packed = (packed + qkv_b[...].astype(jnp.float32)).astype(jnp.bfloat16)
    packed_ref[:, 0:C] = packed[:, 0:C]
    packed_ref[:, 384 : 384 + C] = packed[:, C : 2 * C]
    packed_ref[:, 768 : 768 + C] = packed[:, 2 * C :]
    for window in range(2):
        first = window * WIN
        for group in range(3):
            width = 128 if group < 2 else 64
            heads = width // HD
            lanes = group * 128
            queries = packed_ref[first : first + WIN, lanes : lanes + width]
            keys = packed_ref[first : first + WIN, 384 + lanes : 384 + lanes + width]
            values = packed_ref[first : first + WIN, 768 + lanes : 768 + lanes + width]
            lane_head = lax.broadcasted_iota(jnp.int32, (WIN, width), 1) // HD
            ones = jnp.ones((WIN, width), jnp.bfloat16)
            values = jnp.concatenate([values, ones], axis=1)
            gathered = jnp.zeros((WIN, width), jnp.float32)
            for head in range(heads):
                own = jnp.where(lane_head == head, queries, jnp.zeros_like(queries))
                scores = lax.dot_general(
                    own, keys, (((1,), (1,)), ((), ())), preferred_element_type=jnp.float32
                ) * HD ** (-0.5)
                at = (2 * (group * 4 + head) + window) * WIN
                scores = scores + jnp.concatenate(
                    [addend_ref[0, at : at + WIN, :], addend_ref[1, at : at + WIN, 0 : WIN - 128]],
                    axis=1,
                )
                raised = jnp.exp(scores - jnp.max(scores, axis=-1, keepdims=True))
                mixed = jnp.dot(
                    raised.astype(jnp.bfloat16), values, preferred_element_type=jnp.float32
                )
                mixed = mixed[:, :width] / mixed[:, width:]
                gathered = jnp.where(lane_head == head, mixed, gathered)
            attended_ref[first : first + WIN, lanes : lanes + width] = gathered.astype(jnp.bfloat16)
    for copy in copies[4:]:
        copy.wait()
    mid = (
        field_ref[...]
        + jnp.dot(attended_ref[...], proj_w[0], preferred_element_type=jnp.float32)
        + out_b[0, 0:1].astype(jnp.float32)
    )
    normed_two = layer_norm(mid, ln_g[0, 1:2], ln_s[0, 1:2]).astype(jnp.bfloat16)
    hidden = jnp.dot(normed_two, fc1_w[0], preferred_element_type=jnp.float32)
    hidden = hidden + fc1_b[...].astype(jnp.float32)
    hidden = (hidden * 0.5 * (1.0 + lax.erf(hidden * np.float32(np.sqrt(0.5))))).astype(
        jnp.bfloat16
    )
    field_ref[...] = (
        mid
        + lax.dot_general(
            hidden, fc2_w[0], (((1,), (1,)), ((), ())), preferred_element_type=jnp.float32
        )
        + out_b[0, 1:2].astype(jnp.float32)
    )


def first_kernel(prepares, *refs):
    if prepares:
        patch_hbm, arrange_hbm, hbm, table_hbm, spread_hbm = *refs[:2], refs[2:11], *refs[11:13]
        outs, addend_ref, arrange_ref, params = refs[13:17], refs[17], refs[18], refs[19:28]
        field_ref, packed_ref, attended_ref, quarter_ref = refs[28:32]
        patch_ref, table_ref, spread_ref, wide_ref, rows_ref, sems = refs[32:]
    else:
        patch_ref, arrange_ref, params, addend_ref = *refs[:2], refs[2:11], refs[11]
        outs, (field_ref, packed_ref, attended_ref, quarter_ref) = refs[12:16], refs[16:]

    @pl.when(lax.axis_index("section") == 0)
    def work():
        copies = []
        if prepares:
            copies = fetch(
                (table_hbm, spread_hbm, patch_hbm, arrange_hbm, *hbm),
                (table_ref, spread_ref, patch_ref, arrange_ref, *params),
                sems,
            )
            for copy in copies[:4]:
                copy.wait()
            copies = copies[4:]
            lay_out_bias(table_ref, spread_ref, addend_ref, wide_ref, rows_ref)
        for lat in range(WLAT):
            for lon in range(WLON):
                at = (lat * WLON + lon) * 4
                field_ref[at : at + 4, :] = patch_ref[0, lat, lon].astype(jnp.float32)
        field_ref[...] = jnp.dot(
            arrange_ref[...],
            field_ref[...].astype(jnp.bfloat16),
            preferred_element_type=jnp.float32,
        )
        run_block(field_ref, params, copies, addend_ref, packed_ref, attended_ref)
        for quarter in range(4):
            for place in range(4):
                lev = (place + 1) % 4
                at = (lev // 2) * WIN + quarter * QUARTER + (lev % 2) * PIECE
                quarter_ref[place * PIECE : (place + 1) * PIECE, :] = field_ref[at : at + PIECE, :]
            outs[quarter][...] = pack(quarter_ref)


def second_kernel(*refs):
    quarters, params, addend_ref, outs = refs[:4], refs[4:13], refs[13], refs[14:18]
    field_ref, packed_ref, attended_ref, quarter_ref = refs[18:]

    @pl.when(lax.axis_index("section") == 1)
    def work():
        for quarter in range(4):
            at = quarter * QUARTER
            unpack(quarters[quarter], field_ref, (at, WIN + at))
        run_block(field_ref, params, [], addend_ref, packed_ref, attended_ref)
        for quarter in range(4):
            for window in range(2):
                at = window * WIN + quarter * QUARTER
                quarter_ref[window * QUARTER : (window + 1) * QUARTER, :] = field_ref[
                    at : at + QUARTER, :
                ]
            outs[quarter][...] = pack(quarter_ref)


def place_kernel(*refs):
    arrange_ref, out_ref, grid_ref = refs[8:]

    def place(quarters):
        for at, quarter in enumerate(quarters):
            unpack(quarter, grid_ref, (2 * at * QUARTER, (2 * at + 1) * QUARTER))
        grid_ref[...] = jnp.dot(
            arrange_ref[...],
            grid_ref[...].astype(jnp.bfloat16),
            preferred_element_type=jnp.float32,
        )
        for lat in range(WLAT):
            for lon in range(WLON):
                at = (lat * WLON + lon) * 4
                out_ref[0, lat, lon] = grid_ref[at : at + 4, :].astype(jnp.bfloat16)

    section = lax.axis_index("section")
    pl.when(section == 0)(lambda: place(refs[0:4]))
    pl.when(section == 1)(lambda: place([refs[6], refs[4], refs[7], refs[5]]))


def call(kernel, operands, places, outs, scratch, flops):
    spaces = {"h": pltpu.HBM, "v": pltpu.VMEM}
    operands = [
        pltpu.with_memory_space_constraint(operand, pltpu.HBM) if place == "h" else operand
        for operand, place in zip(operands, places, strict=True)
    ]
    return pl.pallas_call(
        kernel,
        out_shape=outs,
        in_specs=[pl.BlockSpec(memory_space=spaces[place]) for place in places],
        out_specs=jax.tree.map(lambda unused: pl.BlockSpec(memory_space=pltpu.VMEM), outs),
        scratch_shapes=scratch,
        compiler_params=pltpu.CompilerParams(vmem_limit_bytes=VMEM_LIMIT),
        cost_estimate=pl.CostEstimate(flops=flops, bytes_accessed=4_000_000, transcendentals=0),
    )(*operands)


QUARTERS = [jax.ShapeDtypeStruct((5 * QUARTER, 128), jnp.bfloat16)] * 4
BLOCK_SCRATCH = [
    pltpu.VMEM((2 * WIN, C), jnp.float32),
    pltpu.VMEM((2 * WIN, 3 * 384), jnp.bfloat16),
    pltpu.VMEM((2 * WIN, C), jnp.bfloat16),
    pltpu.VMEM((2 * QUARTER, C), jnp.float32),
]
BLOCK_FLOPS = 800_000_000


def held(array):
    return pltpu.VMEM(array.shape, array.dtype)


def mirrored(lon):
    lons = lax.axis_size("lon")
    across = 4 if lons % 4 == 0 else 1
    return (lons // across - 1 - lon // across) * across + lon % across


def straight(lon):
    return lon


def eastward(lon):
    return (lon + 1) % lax.axis_size("lon")


def send(block, sections, steps, source_at, target_at):
    lons, lats = lax.axis_size("lon"), lax.axis_size("lat")
    route = []
    for lon in range(lons):
        for lat in range(lats):
            here = source_at(lon) * lats + lat
            there = target_at((lon + steps[1]) % lons) * lats + (lat + steps[0]) % lats
            route.append((here * 2 + sections[0], there * 2 + sections[1]))
    return lax.ppermute(block, AXES, route)


def to_shifted(quarters, source_at, target_at):
    moved = [
        send(quarters[q], (0, 1), (q // 2 - 1, q % 2 - 1), source_at, target_at) for q in range(4)
    ]
    return [moved[3 - q] for q in range(4)]


def body(
    inputs,
    ln_gain,
    ln_shift,
    qkv_weight,
    qkv_bias,
    proj_weight,
    fc1_weight,
    fc1_bias,
    fc2_weight,
    out_bias,
    bias_table,
):
    params = (
        ln_gain,
        ln_shift,
        qkv_weight,
        qkv_bias,
        proj_weight,
        fc1_weight,
        fc1_bias,
        fc2_weight,
        out_bias,
    )
    params = (*params[:7], fc2_weight.transpose(0, 2, 1), out_bias)
    patch = inputs.transpose(0, 2, 3, 1, 4)
    table = bias_table.transpose(0, 2, 3, 1, 4)
    other = send(patch, (1, 0), (0, 0), straight, mirrored)
    arrange = jnp.asarray(arrange_matrix())
    spread = jnp.asarray(spread_matrix())
    addend_shape = jax.ShapeDtypeStruct((2, 2 * HEADS * WIN, 128), jnp.float32)
    bias_scratch = [
        held(table),
        held(spread),
        pltpu.VMEM((24, table.shape[-1]), jnp.float32),
        pltpu.VMEM((12 * 24, spread.shape[0]), jnp.float32),
    ]
    brought = [jax.ShapeDtypeStruct(member.shape, member.dtype) for member in params]
    made = call(
        functools.partial(first_kernel, True),
        (patch, arrange, *params, table, spread),
        "h" * 13,
        [*QUARTERS, addend_shape, jax.ShapeDtypeStruct(arrange.shape, arrange.dtype), *brought],
        [*BLOCK_SCRATCH, held(patch), *bias_scratch, pltpu.SemaphoreType.DMA((13,))],
        BLOCK_FLOPS,
    )
    own_first, (addend_one, arranging), params_one = made[:4], made[4:6], made[6:]
    own_shifted = to_shifted(own_first, straight, mirrored)
    addend_two, *params_two = call(
        prepare_kernel,
        (table, spread, *params, own_first[0]),
        "h" * 11 + "v",
        [addend_shape, *brought],
        [*bias_scratch, pltpu.SemaphoreType.DMA((11,))],
        200_000_000,
    )
    other_first = call(
        functools.partial(first_kernel, False),
        (other, arranging, *params_one, addend_one),
        "v" * 12,
        QUARTERS,
        BLOCK_SCRATCH,
        BLOCK_FLOPS,
    )
    other_shifted = to_shifted(other_first, mirrored, eastward)
    block_two = functools.partial(
        call,
        second_kernel,
        places="v" * 14,
        outs=QUARTERS,
        scratch=BLOCK_SCRATCH,
        flops=BLOCK_FLOPS,
    )
    own_done = block_two((*own_shifted, *params_two, addend_two))
    own_back = [
        send(own_done[3 - q], (1, 0), (1 - q // 2, 1 - q % 2), mirrored, straight)
        for q in range(4)
    ]
    other_done = block_two((*other_shifted, *params_two, addend_two))
    across, along, upward = [
        send(other_done[3 - q], (1, 1), (1 - q // 2, 1 - q % 2), eastward, straight)
        for q in (1, 3, 0)
    ]
    placed = call(
        place_kernel,
        (*own_back, across, along, upward, other_done[1], jnp.asarray(place_matrix())),
        "v" * 9,
        jax.ShapeDtypeStruct(patch.shape, patch.dtype),
        [pltpu.VMEM((2 * WIN, C), jnp.float32)],
        1_000_000,
    )
    return placed.transpose(0, 3, 1, 2, 4)


def solution(mesh):
    return jax.shard_map(
        body,
        mesh=mesh,
        in_specs=(
            P("section", None, "lat", "lon", None),
            P("section", None, None),
            P("section", None, None),
            P("section", None, None),
            P("section", None),
            P("section", None, None),
            P("section", None, None),
            P("section", None),
            P("section", None, None),
            P("section", None, None),
            P("section", None, "lat", None, None),
        ),
        out_specs=P("section", None, "lat", "lon", None),
        check_vma=False,
    )
```

```python
import functools

import jax
import jax.numpy as jnp
import numpy as np
from jax import lax
from jax.experimental import pallas as pl
from jax.experimental.pallas import tpu as pltpu
from jax.sharding import PartitionSpec as P

HD = 32
HEADS = 10
C = 320
WLEV = 2
WLAT = 6
WLON = 12
WIN = WLEV * WLAT * WLON
QUARTER = WIN // 4
PIECE = QUARTER // WLEV
SPAN = 2 * WLON - 1
AXES = ("lon", "lat", "section")
VMEM_LIMIT = 20 * 1024 * 1024


def token_row(lev, lat, lon):
    quarter = (lat // 3) * 2 + lon // 6
    return quarter * QUARTER + lev * PIECE + (lat % 3) * 6 + lon % 6


def spread_matrix():
    spread = np.zeros((WLEV * WLAT * SPAN, WLON, 256), np.float32)
    for lev in range(WLEV):
        for lat in range(WLAT):
            for lon in range(WLON):
                for query_lon in range(WLON):
                    source = (lev * WLAT + lat) * SPAN + query_lon - lon + WLON - 1
                    spread[source, query_lon, token_row(lev, lat, lon)] = 1.0
    return spread.reshape(WLEV * WLAT * SPAN, WLON * 256).astype(jnp.bfloat16)


def arrange_matrix():
    arrange = np.zeros((2 * WIN, 2 * WIN), np.float32)
    for lev in range(4):
        for lat in range(WLAT):
            for lon in range(WLON):
                row = (lev // 2) * WIN + token_row(lev % 2, lat, lon)
                arrange[row, (lat * WLON + lon) * 4 + lev] = 1.0
    return arrange.astype(jnp.bfloat16)


def place_matrix():
    arrange = np.zeros((2 * WIN, 2 * WIN), np.float32)
    for lev in range(4):
        for lat in range(WLAT):
            for lon in range(WLON):
                quarter = (lat // 3) * 2 + lon // 6
                source = ((quarter * 4 + (lev + 3) % 4) * 3 + lat % 3) * 6 + lon % 6
                arrange[(lat * WLON + lon) * 4 + lev, source] = 1.0
    return arrange.astype(jnp.bfloat16)


def lay_out_bias(table_ref, spread_ref, addend_ref, wide_ref, rows_ref):
    for head in range(HEADS):
        wide_ref[2 * head : 2 * head + 2, :] = table_ref[0, 0, head].astype(jnp.float32)
    for lev in range(WLEV):
        for lat in range(WLAT):
            parts = []
            for key_lev in range(WLEV):
                for key_lat in range(WLAT):
                    at = ((key_lev * WLEV + lev) * WLAT * WLAT + key_lat * WLAT + lat) * SPAN
                    parts.append(wide_ref[:, at : at + SPAN])
            first = (lev * WLAT + lat) * 24
            rows_ref[first : first + 24, :] = jnp.concatenate(parts, axis=1)
    rows = rows_ref[...].astype(jnp.bfloat16)
    for lon in range(WLON):
        dense = jnp.dot(
            rows, spread_ref[:, lon * 256 : lon * 256 + 256], preferred_element_type=jnp.float32
        )
        for lev in range(WLEV):
            for lat in range(WLAT):
                first = (lev * WLAT + lat) * 24
                row = token_row(lev, lat, lon)
                for tile in range(2):
                    addend_ref[tile, pl.ds(row, 2 * HEADS, stride=WIN), :] = dense[
                        first : first + 2 * HEADS, tile * 128 : tile * 128 + 128
                    ]


def fetch(sources, targets, sems):
    copies = [
        pltpu.make_async_copy(source, target, sems.at[at])
        for at, (source, target) in enumerate(zip(sources, targets, strict=True))
    ]
    for copy in copies:
        copy.start()
    return copies


def pack(quarter_ref):
    rest = jnp.concatenate(
        [quarter_ref[0:QUARTER, 256:C], quarter_ref[QUARTER : 2 * QUARTER, 256:C]], axis=1
    )
    return jnp.concatenate(
        [quarter_ref[:, 0:128], quarter_ref[:, 128:256], rest], axis=0
    ).astype(jnp.bfloat16)


def unpack(packed_ref, target_ref, starts):
    packed = packed_ref[...].astype(jnp.float32)
    for half, at in enumerate(starts):
        rows = slice(at, at + QUARTER)
        target_ref[rows, 0:128] = packed[half * QUARTER : (half + 1) * QUARTER]
        target_ref[rows, 128:256] = packed[(2 + half) * QUARTER : (3 + half) * QUARTER]
        target_ref[rows, 256:C] = packed[4 * QUARTER :, half * 64 : half * 64 + 64]


def prepare_kernel(*refs):
    table_hbm, spread_hbm, hbm = refs[0], refs[1], refs[2:11]
    addend_ref, params = refs[12], refs[13:22]
    table_ref, spread_ref, wide_ref, rows_ref, sems = refs[22:]
    last_lat = lax.axis_index("lat") == lax.axis_size("lat") - 1

    @pl.when(lax.axis_index("section") == 1)
    def work():
        copies = fetch(
            (table_hbm, spread_hbm, *hbm), (table_ref, spread_ref, *params), sems
        )
        for copy in copies:
            copy.wait()
        lay_out_bias(table_ref, spread_ref, addend_ref, wide_ref, rows_ref)
        for tile in range(2):
            query = lax.broadcasted_iota(jnp.int32, (WIN, 128), 0)
            key = lax.broadcasted_iota(jnp.int32, (WIN, 128), 1) + tile * 128
            lat_differs = jnp.logical_and((query >= 2 * QUARTER) != (key >= 2 * QUARTER), last_lat)
            lev_differs = (query % QUARTER >= PIECE) != (key % QUARTER >= PIECE)
            for window in range(2):
                barred = jnp.logical_or(lat_differs, lev_differs) if window else lat_differs
                for head in range(HEADS):
                    at = (2 * head + window) * WIN
                    addend_ref[tile, at : at + WIN, :] = jnp.where(
                        barred, jnp.float32(-1e30), addend_ref[tile, at : at + WIN, :]
                    )


def layer_norm(values, norm_gain, norm_shift):
    center = values - jnp.mean(values, axis=-1, keepdims=True)
    spread = jnp.mean(center * center, axis=-1, keepdims=True)
    return center * lax.rsqrt(spread + 1e-05) * norm_gain.astype(jnp.float32) + norm_shift.astype(
        jnp.float32
    )


def run_block(field_ref, params, copies, addend_ref, packed_ref, attended_ref):
    ln_g, ln_s, qkv_w, qkv_b, proj_w, fc1_w, fc1_b, fc2_w, out_b = params
    for copy in copies[:4]:
        copy.wait()
    normed = layer_norm(field_ref[...], ln_g[0, 0:1], ln_s[0, 0:1]).astype(jnp.bfloat16)
    packed = jnp.dot(normed, qkv_w[0], preferred_element_type=jnp.float32)
    packed = (packed + qkv_b[...].astype(jnp.float32)).astype(jnp.bfloat16)
    packed_ref[:, 0:C] = packed[:, 0:C]
    packed_ref[:, 384 : 384 + C] = packed[:, C : 2 * C]
    packed_ref[:, 768 : 768 + C] = packed[:, 2 * C :]
    for window in range(2):
        first = window * WIN
        for group in range(3):
            width = 128 if group < 2 else 64
            heads = width // HD
            lanes = group * 128
            queries = packed_ref[first : first + WIN, lanes : lanes + width]
            keys = packed_ref[first : first + WIN, 384 + lanes : 384 + lanes + width]
            values = packed_ref[first : first + WIN, 768 + lanes : 768 + lanes + width]
            lane_head = lax.broadcasted_iota(jnp.int32, (WIN, width), 1) // HD
            ones = jnp.ones((WIN, width), jnp.bfloat16)
            values = jnp.concatenate([values, ones], axis=1)
            gathered = jnp.zeros((WIN, width), jnp.float32)
            for head in range(heads):
                own = jnp.where(lane_head == head, queries, jnp.zeros_like(queries))
                scores = lax.dot_general(
                    own, keys, (((1,), (1,)), ((), ())), preferred_element_type=jnp.float32
                ) * HD ** (-0.5)
                at = (2 * (group * 4 + head) + window) * WIN
                scores = scores + jnp.concatenate(
                    [addend_ref[0, at : at + WIN, :], addend_ref[1, at : at + WIN, 0 : WIN - 128]],
                    axis=1,
                )
                raised = jnp.exp(scores - jnp.max(scores, axis=-1, keepdims=True))
                mixed = jnp.dot(
                    raised.astype(jnp.bfloat16), values, preferred_element_type=jnp.float32
                )
                mixed = mixed[:, :width] / mixed[:, width:]
                gathered = jnp.where(lane_head == head, mixed, gathered)
            attended_ref[first : first + WIN, lanes : lanes + width] = gathered.astype(jnp.bfloat16)
    for copy in copies[4:]:
        copy.wait()
    mid = (
        field_ref[...]
        + jnp.dot(attended_ref[...], proj_w[0], preferred_element_type=jnp.float32)
        + out_b[0, 0:1].astype(jnp.float32)
    )
    normed_two = layer_norm(mid, ln_g[0, 1:2], ln_s[0, 1:2]).astype(jnp.bfloat16)
    hidden = jnp.dot(normed_two, fc1_w[0], preferred_element_type=jnp.float32)
    hidden = hidden + fc1_b[...].astype(jnp.float32)
    hidden = (hidden * 0.5 * (1.0 + lax.erf(hidden * np.float32(np.sqrt(0.5))))).astype(
        jnp.bfloat16
    )
    field_ref[...] = (
        mid
        + lax.dot_general(
            hidden, fc2_w[0], (((1,), (1,)), ((), ())), preferred_element_type=jnp.float32
        )
        + out_b[0, 1:2].astype(jnp.float32)
    )


def first_kernel(prepares, *refs):
    if prepares:
        patch_hbm, arrange_hbm, hbm, table_hbm, spread_hbm = *refs[:2], refs[2:11], *refs[11:13]
        outs, addend_ref, arrange_ref, params = refs[13:17], refs[17], refs[18], refs[19:28]
        field_ref, packed_ref, attended_ref, quarter_ref = refs[28:32]
        patch_ref, table_ref, spread_ref, wide_ref, rows_ref, sems = refs[32:]
    else:
        patch_ref, arrange_ref, params, addend_ref = *refs[:2], refs[2:11], refs[11]
        outs, (field_ref, packed_ref, attended_ref, quarter_ref) = refs[12:16], refs[16:]

    @pl.when(lax.axis_index("section") == 0)
    def work():
        copies = []
        if prepares:
            copies = fetch(
                (table_hbm, spread_hbm, patch_hbm, arrange_hbm, *hbm),
                (table_ref, spread_ref, patch_ref, arrange_ref, *params),
                sems,
            )
            for copy in copies[:4]:
                copy.wait()
            copies = copies[4:]
            lay_out_bias(table_ref, spread_ref, addend_ref, wide_ref, rows_ref)
        for lat in range(WLAT):
            for lon in range(WLON):
                at = (lat * WLON + lon) * 4
                field_ref[at : at + 4, :] = patch_ref[0, lat, lon].astype(jnp.float32)
        field_ref[...] = jnp.dot(
            arrange_ref[...],
            field_ref[...].astype(jnp.bfloat16),
            preferred_element_type=jnp.float32,
        )
        run_block(field_ref, params, copies, addend_ref, packed_ref, attended_ref)
        for quarter in range(4):
            for place in range(4):
                lev = (place + 1) % 4
                at = (lev // 2) * WIN + quarter * QUARTER + (lev % 2) * PIECE
                quarter_ref[place * PIECE : (place + 1) * PIECE, :] = field_ref[at : at + PIECE, :]
            outs[quarter][...] = pack(quarter_ref)


def second_kernel(*refs):
    quarters, params, addend_ref, outs = refs[:4], refs[4:13], refs[13], refs[14:18]
    field_ref, packed_ref, attended_ref, quarter_ref = refs[18:]

    @pl.when(lax.axis_index("section") == 1)
    def work():
        for quarter in range(4):
            at = quarter * QUARTER
            unpack(quarters[quarter], field_ref, (at, WIN + at))
        run_block(field_ref, params, [], addend_ref, packed_ref, attended_ref)
        for quarter in range(4):
            for window in range(2):
                at = window * WIN + quarter * QUARTER
                quarter_ref[window * QUARTER : (window + 1) * QUARTER, :] = field_ref[
                    at : at + QUARTER, :
                ]
            outs[quarter][...] = pack(quarter_ref)


def place_kernel(*refs):
    arrange_ref, out_ref, grid_ref = refs[8:]

    def place(quarters):
        for at, quarter in enumerate(quarters):
            unpack(quarter, grid_ref, (2 * at * QUARTER, (2 * at + 1) * QUARTER))
        grid_ref[...] = jnp.dot(
            arrange_ref[...],
            grid_ref[...].astype(jnp.bfloat16),
            preferred_element_type=jnp.float32,
        )
        for lat in range(WLAT):
            for lon in range(WLON):
                at = (lat * WLON + lon) * 4
                out_ref[0, lat, lon] = grid_ref[at : at + 4, :].astype(jnp.bfloat16)

    section = lax.axis_index("section")
    pl.when(section == 0)(lambda: place(refs[0:4]))
    pl.when(section == 1)(lambda: place([refs[6], refs[4], refs[7], refs[5]]))


def call(kernel, operands, places, outs, scratch, flops):
    spaces = {"h": pltpu.HBM, "v": pltpu.VMEM}
    operands = [
        pltpu.with_memory_space_constraint(operand, pltpu.HBM) if place == "h" else operand
        for operand, place in zip(operands, places, strict=True)
    ]
    return pl.pallas_call(
        kernel,
        out_shape=outs,
        in_specs=[pl.BlockSpec(memory_space=spaces[place]) for place in places],
        out_specs=jax.tree.map(lambda unused: pl.BlockSpec(memory_space=pltpu.VMEM), outs),
        scratch_shapes=scratch,
        compiler_params=pltpu.CompilerParams(vmem_limit_bytes=VMEM_LIMIT),
        cost_estimate=pl.CostEstimate(flops=flops, bytes_accessed=4_000_000, transcendentals=0),
    )(*operands)


QUARTERS = [jax.ShapeDtypeStruct((5 * QUARTER, 128), jnp.bfloat16)] * 4
BLOCK_SCRATCH = [
    pltpu.VMEM((2 * WIN, C), jnp.float32),
    pltpu.VMEM((2 * WIN, 3 * 384), jnp.bfloat16),
    pltpu.VMEM((2 * WIN, C), jnp.bfloat16),
    pltpu.VMEM((2 * QUARTER, C), jnp.float32),
]
BLOCK_FLOPS = 800_000_000


def held(array):
    return pltpu.VMEM(array.shape, array.dtype)


def mirrored(lon):
    lons = lax.axis_size("lon")
    across = 4 if lons % 4 == 0 else 1
    return (lons // across - 1 - lon // across) * across + lon % across


def straight(lon):
    return lon


def eastward(lon):
    return (lon + 1) % lax.axis_size("lon")


def mirrored_eastward(lon):
    return mirrored(eastward(lon))


def send(block, sections, steps, source_at, target_at):
    lons, lats = lax.axis_size("lon"), lax.axis_size("lat")
    route = []
    for lon in range(lons):
        for lat in range(lats):
            here = source_at(lon) * lats + lat
            there = target_at((lon + steps[1]) % lons) * lats + (lat + steps[0]) % lats
            route.append((here * 2 + sections[0], there * 2 + sections[1]))
    return lax.ppermute(block, AXES, route)


def to_shifted(quarters, source_at, target_at):
    moved = [
        send(quarters[q], (0, 1), (q // 2 - 1, q % 2 - 1), source_at, target_at) for q in range(4)
    ]
    return [moved[3 - q] for q in range(4)]


def body(
    inputs,
    ln_gain,
    ln_shift,
    qkv_weight,
    qkv_bias,
    proj_weight,
    fc1_weight,
    fc1_bias,
    fc2_weight,
    out_bias,
    bias_table,
):
    params = (
        ln_gain,
        ln_shift,
        qkv_weight,
        qkv_bias,
        proj_weight,
        fc1_weight,
        fc1_bias,
        fc2_weight,
        out_bias,
    )
    params = (*params[:7], fc2_weight.transpose(0, 2, 1), out_bias)
    patch = inputs.transpose(0, 2, 3, 1, 4)
    table = bias_table.transpose(0, 2, 3, 1, 4)
    other = send(patch, (1, 0), (0, 0), straight, mirrored)
    arrange = jnp.asarray(arrange_matrix())
    spread = jnp.asarray(spread_matrix())
    addend_shape = jax.ShapeDtypeStruct((2, 2 * HEADS * WIN, 128), jnp.float32)
    bias_scratch = [
        held(table),
        held(spread),
        pltpu.VMEM((24, table.shape[-1]), jnp.float32),
        pltpu.VMEM((12 * 24, spread.shape[0]), jnp.float32),
    ]
    brought = [jax.ShapeDtypeStruct(member.shape, member.dtype) for member in params]
    made = call(
        functools.partial(first_kernel, True),
        (patch, arrange, *params, table, spread),
        "h" * 13,
        [*QUARTERS, addend_shape, jax.ShapeDtypeStruct(arrange.shape, arrange.dtype), *brought],
        [*BLOCK_SCRATCH, held(patch), *bias_scratch, pltpu.SemaphoreType.DMA((13,))],
        BLOCK_FLOPS,
    )
    own_first, (addend_one, arranging), params_one = made[:4], made[4:6], made[6:]
    own_shifted = to_shifted(own_first, straight, mirrored_eastward)
    addend_two, *params_two = call(
        prepare_kernel,
        (table, spread, *params, own_first[0]),
        "h" * 11 + "v",
        [addend_shape, *brought],
        [*bias_scratch, pltpu.SemaphoreType.DMA((11,))],
        200_000_000,
    )
    other_first = call(
        functools.partial(first_kernel, False),
        (other, arranging, *params_one, addend_one),
        "v" * 12,
        QUARTERS,
        BLOCK_SCRATCH,
        BLOCK_FLOPS,
    )
    other_shifted = to_shifted(other_first, mirrored, eastward)
    block_two = functools.partial(
        call,
        second_kernel,
        places="v" * 14,
        outs=QUARTERS,
        scratch=BLOCK_SCRATCH,
        flops=BLOCK_FLOPS,
    )
    own_done = block_two((*own_shifted, *params_two, addend_two))
    own_back = [
        send(own_done[3 - q], (1, 0), (1 - q // 2, 1 - q % 2), mirrored_eastward, straight)
        for q in range(4)
    ]
    other_done = block_two((*other_shifted, *params_two, addend_two))
    across, along, upward = [
        send(other_done[3 - q], (1, 1), (1 - q // 2, 1 - q % 2), eastward, straight)
        for q in (1, 3, 0)
    ]
    placed = call(
        place_kernel,
        (*own_back, across, along, upward, other_done[1], jnp.asarray(place_matrix())),
        "v" * 9,
        jax.ShapeDtypeStruct(patch.shape, patch.dtype),
        [pltpu.VMEM((2 * WIN, C), jnp.float32)],
        1_000_000,
    )
    return placed.transpose(0, 3, 1, 2, 4)


def solution(mesh):
    return jax.shard_map(
        body,
        mesh=mesh,
        in_specs=(
            P("section", None, "lat", "lon", None),
            P("section", None, None),
            P("section", None, None),
            P("section", None, None),
            P("section", None),
            P("section", None, None),
            P("section", None, None),
            P("section", None),
            P("section", None, None),
            P("section", None, None),
            P("section", None, "lat", None, None),
        ),
        out_specs=P("section", None, "lat", "lon", None),
        check_vma=False,
    )
```

```python
import functools

import jax
import jax.numpy as jnp
import numpy as np
from jax import lax
from jax.experimental import pallas as pl
from jax.experimental.pallas import tpu as pltpu
from jax.sharding import PartitionSpec as P

HD = 32
HEADS = 10
C = 320
WLEV = 2
WLAT = 6
WLON = 12
WIN = WLEV * WLAT * WLON
QUARTER = WIN // 4
PIECE = QUARTER // WLEV
SPAN = 2 * WLON - 1
AXES = ("lon", "lat", "section")
VMEM_LIMIT = 20 * 1024 * 1024


def token_row(lev, lat, lon):
    quarter = (lat // 3) * 2 + lon // 6
    return quarter * QUARTER + lev * PIECE + (lat % 3) * 6 + lon % 6


def spread_matrix():
    spread = np.zeros((WLEV * WLAT * SPAN, WLON, 256), np.float32)
    for lev in range(WLEV):
        for lat in range(WLAT):
            for lon in range(WLON):
                for query_lon in range(WLON):
                    source = (lev * WLAT + lat) * SPAN + query_lon - lon + WLON - 1
                    spread[source, query_lon, token_row(lev, lat, lon)] = 1.0
    return spread.reshape(WLEV * WLAT * SPAN, WLON * 256).astype(jnp.bfloat16)


def arrange_matrix():
    arrange = np.zeros((2 * WIN, 2 * WIN), np.float32)
    for lev in range(4):
        for lat in range(WLAT):
            for lon in range(WLON):
                row = (lev // 2) * WIN + token_row(lev % 2, lat, lon)
                arrange[row, (lat * WLON + lon) * 4 + lev] = 1.0
    return arrange.astype(jnp.bfloat16)


def place_matrix():
    arrange = np.zeros((2 * WIN, 2 * WIN), np.float32)
    for lev in range(4):
        for lat in range(WLAT):
            for lon in range(WLON):
                quarter = (lat // 3) * 2 + lon // 6
                source = ((quarter * 4 + (lev + 3) % 4) * 3 + lat % 3) * 6 + lon % 6
                arrange[(lat * WLON + lon) * 4 + lev, source] = 1.0
    return arrange.astype(jnp.bfloat16)


def lay_out_bias(table_ref, spread_ref, addend_ref, wide_ref, rows_ref):
    for head in range(HEADS):
        both = table_ref[0, 0, head].astype(jnp.float32)
        for window in range(2):
            at = window * HEADS + head
            wide_ref[at : at + 1, :] = both[window : window + 1]
    for lev in range(WLEV):
        for lat in range(WLAT):
            parts = []
            for key_lev in range(WLEV):
                for key_lat in range(WLAT):
                    at = ((key_lev * WLEV + lev) * WLAT * WLAT + key_lat * WLAT + lat) * SPAN
                    parts.append(wide_ref[:, at : at + SPAN])
            first = (lev * WLAT + lat) * 24
            rows_ref[first : first + 24, :] = jnp.concatenate(parts, axis=1)
    rows = rows_ref[...].astype(jnp.bfloat16)
    for lon in range(WLON):
        dense = jnp.dot(
            rows, spread_ref[:, lon * 256 : lon * 256 + 256], preferred_element_type=jnp.float32
        )
        for lev in range(WLEV):
            for lat in range(WLAT):
                first = (lev * WLAT + lat) * 24
                row = token_row(lev, lat, lon)
                for tile in range(2):
                    addend_ref[tile, pl.ds(row, 2 * HEADS, stride=WIN), :] = dense[
                        first : first + 2 * HEADS, tile * 128 : tile * 128 + 128
                    ]


def fetch(sources, targets, sems):
    copies = [
        pltpu.make_async_copy(source, target, sems.at[at])
        for at, (source, target) in enumerate(zip(sources, targets, strict=True))
    ]
    for copy in copies:
        copy.start()
    return copies


def pack(quarter_ref):
    rest = jnp.concatenate(
        [quarter_ref[0:QUARTER, 256:C], quarter_ref[QUARTER : 2 * QUARTER, 256:C]], axis=1
    )
    return jnp.concatenate(
        [quarter_ref[:, 0:128], quarter_ref[:, 128:256], rest], axis=0
    ).astype(jnp.bfloat16)


def unpack(packed_ref, target_ref, starts):
    packed = packed_ref[...].astype(jnp.float32)
    for half, at in enumerate(starts):
        rows = slice(at, at + QUARTER)
        target_ref[rows, 0:128] = packed[half * QUARTER : (half + 1) * QUARTER]
        target_ref[rows, 128:256] = packed[(2 + half) * QUARTER : (3 + half) * QUARTER]
        target_ref[rows, 256:C] = packed[4 * QUARTER :, half * 64 : half * 64 + 64]


def prepare_kernel(*refs):
    table_hbm, spread_hbm, hbm = refs[0], refs[1], refs[2:11]
    addend_ref, params = refs[12], refs[13:22]
    table_ref, spread_ref, wide_ref, rows_ref, sems = refs[22:]
    last_lat = lax.axis_index("lat") == lax.axis_size("lat") - 1

    @pl.when(lax.axis_index("section") == 1)
    def work():
        copies = fetch(
            (table_hbm, spread_hbm, *hbm), (table_ref, spread_ref, *params), sems
        )
        for copy in copies:
            copy.wait()
        lay_out_bias(table_ref, spread_ref, addend_ref, wide_ref, rows_ref)
        for tile in range(2):
            query = lax.broadcasted_iota(jnp.int32, (WIN, 128), 0)
            key = lax.broadcasted_iota(jnp.int32, (WIN, 128), 1) + tile * 128
            lat_differs = jnp.logical_and((query >= 2 * QUARTER) != (key >= 2 * QUARTER), last_lat)
            lev_differs = (query % QUARTER >= PIECE) != (key % QUARTER >= PIECE)
            for window in range(2):
                barred = jnp.logical_or(lat_differs, lev_differs) if window else lat_differs
                for head in range(HEADS):
                    at = (window * HEADS + head) * WIN
                    addend_ref[tile, at : at + WIN, :] = jnp.where(
                        barred, jnp.float32(-1e30), addend_ref[tile, at : at + WIN, :]
                    )


def layer_norm(values, norm_gain, norm_shift):
    center = values - jnp.mean(values, axis=-1, keepdims=True)
    spread = jnp.mean(center * center, axis=-1, keepdims=True)
    return center * lax.rsqrt(spread + 1e-05) * norm_gain.astype(jnp.float32) + norm_shift.astype(
        jnp.float32
    )


def run_block(field_ref, params, copies, addend_ref, packed_ref, attended_ref):
    ln_g, ln_s, qkv_w, qkv_b, proj_w, fc1_w, fc1_b, fc2_w, out_b = params
    for copy in copies[:4]:
        copy.wait()
    normed = layer_norm(field_ref[...], ln_g[0, 0:1], ln_s[0, 0:1]).astype(jnp.bfloat16)
    packed = jnp.dot(normed, qkv_w[0], preferred_element_type=jnp.float32)
    packed = (packed + qkv_b[...].astype(jnp.float32)).astype(jnp.bfloat16)
    packed_ref[:, 0:C] = packed[:, 0:C]
    packed_ref[:, 384 : 384 + C] = packed[:, C : 2 * C]
    packed_ref[:, 768 : 768 + C] = packed[:, 2 * C :]
    for window in range(2):
        first = window * WIN
        for group in range(3):
            width = 128 if group < 2 else 64
            heads = width // HD
            lanes = group * 128
            queries = packed_ref[first : first + WIN, lanes : lanes + width]
            keys = packed_ref[first : first + WIN, 384 + lanes : 384 + lanes + width]
            values = packed_ref[first : first + WIN, 768 + lanes : 768 + lanes + width]
            lane_head = lax.broadcasted_iota(jnp.int32, (WIN, width), 1) // HD
            ones = jnp.ones((WIN, width), jnp.bfloat16)
            values = jnp.concatenate([values, ones], axis=1)
            own = [
                jnp.where(lane_head == head, queries, jnp.zeros_like(queries))
                for head in range(heads)
            ]
            scores = lax.dot_general(
                jnp.concatenate(own, axis=0),
                keys,
                (((1,), (1,)), ((), ())),
                preferred_element_type=jnp.float32,
            ) * HD ** (-0.5)
            at = (window * HEADS + group * 4) * WIN
            rows = slice(at, at + heads * WIN)
            scores = scores + jnp.concatenate(
                [addend_ref[0, rows, :], addend_ref[1, rows, 0 : WIN - 128]], axis=1
            )
            raised = jnp.exp(scores - jnp.max(scores, axis=-1, keepdims=True))
            mixed = jnp.dot(raised.astype(jnp.bfloat16), values, preferred_element_type=jnp.float32)
            gathered, sums = mixed[0:WIN, :width], mixed[0:WIN, width:]
            for head in range(1, heads):
                part = mixed[head * WIN : (head + 1) * WIN]
                gathered = jnp.where(lane_head == head, part[:, :width], gathered)
                sums = jnp.where(lane_head == head, part[:, width:], sums)
            gathered = gathered / sums
            attended_ref[first : first + WIN, lanes : lanes + width] = gathered.astype(jnp.bfloat16)
    for copy in copies[4:]:
        copy.wait()
    mid = (
        field_ref[...]
        + jnp.dot(attended_ref[...], proj_w[0], preferred_element_type=jnp.float32)
        + out_b[0, 0:1].astype(jnp.float32)
    )
    normed_two = layer_norm(mid, ln_g[0, 1:2], ln_s[0, 1:2]).astype(jnp.bfloat16)
    hidden = jnp.dot(normed_two, fc1_w[0], preferred_element_type=jnp.float32)
    hidden = hidden + fc1_b[...].astype(jnp.float32)
    hidden = (hidden * 0.5 * (1.0 + lax.erf(hidden * np.float32(np.sqrt(0.5))))).astype(
        jnp.bfloat16
    )
    field_ref[...] = (
        mid
        + lax.dot_general(
            hidden, fc2_w[0], (((1,), (1,)), ((), ())), preferred_element_type=jnp.float32
        )
        + out_b[0, 1:2].astype(jnp.float32)
    )


def first_kernel(prepares, *refs):
    if prepares:
        patch_hbm, arrange_hbm, hbm, table_hbm, spread_hbm = *refs[:2], refs[2:11], *refs[11:13]
        outs, addend_ref, arrange_ref, params = refs[13:17], refs[17], refs[18], refs[19:28]
        field_ref, packed_ref, attended_ref, quarter_ref = refs[28:32]
        patch_ref, table_ref, spread_ref, wide_ref, rows_ref, sems = refs[32:]
    else:
        patch_ref, arrange_ref, params, addend_ref = *refs[:2], refs[2:11], refs[11]
        outs, (field_ref, packed_ref, attended_ref, quarter_ref) = refs[12:16], refs[16:]

    @pl.when(lax.axis_index("section") == 0)
    def work():
        copies = []
        if prepares:
            copies = fetch(
                (table_hbm, spread_hbm, patch_hbm, arrange_hbm, *hbm),
                (table_ref, spread_ref, patch_ref, arrange_ref, *params),
                sems,
            )
            for copy in copies[:4]:
                copy.wait()
            copies = copies[4:]
            lay_out_bias(table_ref, spread_ref, addend_ref, wide_ref, rows_ref)
        for lat in range(WLAT):
            for lon in range(WLON):
                at = (lat * WLON + lon) * 4
                field_ref[at : at + 4, :] = patch_ref[0, lat, lon].astype(jnp.float32)
        field_ref[...] = jnp.dot(
            arrange_ref[...],
            field_ref[...].astype(jnp.bfloat16),
            preferred_element_type=jnp.float32,
        )
        run_block(field_ref, params, copies, addend_ref, packed_ref, attended_ref)
        for quarter in range(4):
            for place in range(4):
                lev = (place + 1) % 4
                at = (lev // 2) * WIN + quarter * QUARTER + (lev % 2) * PIECE
                quarter_ref[place * PIECE : (place + 1) * PIECE, :] = field_ref[at : at + PIECE, :]
            outs[quarter][...] = pack(quarter_ref)


def second_kernel(*refs):
    quarters, params, addend_ref, outs = refs[:4], refs[4:13], refs[13], refs[14:18]
    field_ref, packed_ref, attended_ref, quarter_ref = refs[18:]

    @pl.when(lax.axis_index("section") == 1)
    def work():
        for quarter in range(4):
            at = quarter * QUARTER
            unpack(quarters[quarter], field_ref, (at, WIN + at))
        run_block(field_ref, params, [], addend_ref, packed_ref, attended_ref)
        for quarter in range(4):
            for window in range(2):
                at = window * WIN + quarter * QUARTER
                quarter_ref[window * QUARTER : (window + 1) * QUARTER, :] = field_ref[
                    at : at + QUARTER, :
                ]
            outs[quarter][...] = pack(quarter_ref)


def place_kernel(*refs):
    arrange_ref, out_ref, grid_ref = refs[8:]

    def place(quarters):
        for at, quarter in enumerate(quarters):
            unpack(quarter, grid_ref, (2 * at * QUARTER, (2 * at + 1) * QUARTER))
        grid_ref[...] = jnp.dot(
            arrange_ref[...],
            grid_ref[...].astype(jnp.bfloat16),
            preferred_element_type=jnp.float32,
        )
        for lat in range(WLAT):
            for lon in range(WLON):
                at = (lat * WLON + lon) * 4
                out_ref[0, lat, lon] = grid_ref[at : at + 4, :].astype(jnp.bfloat16)

    section = lax.axis_index("section")
    pl.when(section == 0)(lambda: place(refs[0:4]))
    pl.when(section == 1)(lambda: place([refs[6], refs[4], refs[7], refs[5]]))


def call(kernel, operands, places, outs, scratch, flops):
    spaces = {"h": pltpu.HBM, "v": pltpu.VMEM}
    operands = [
        pltpu.with_memory_space_constraint(operand, pltpu.HBM) if place == "h" else operand
        for operand, place in zip(operands, places, strict=True)
    ]
    return pl.pallas_call(
        kernel,
        out_shape=outs,
        in_specs=[pl.BlockSpec(memory_space=spaces[place]) for place in places],
        out_specs=jax.tree.map(lambda unused: pl.BlockSpec(memory_space=pltpu.VMEM), outs),
        scratch_shapes=scratch,
        compiler_params=pltpu.CompilerParams(vmem_limit_bytes=VMEM_LIMIT),
        cost_estimate=pl.CostEstimate(flops=flops, bytes_accessed=4_000_000, transcendentals=0),
    )(*operands)


QUARTERS = [jax.ShapeDtypeStruct((5 * QUARTER, 128), jnp.bfloat16)] * 4
BLOCK_SCRATCH = [
    pltpu.VMEM((2 * WIN, C), jnp.float32),
    pltpu.VMEM((2 * WIN, 3 * 384), jnp.bfloat16),
    pltpu.VMEM((2 * WIN, C), jnp.bfloat16),
    pltpu.VMEM((2 * QUARTER, C), jnp.float32),
]
BLOCK_FLOPS = 800_000_000


def held(array):
    return pltpu.VMEM(array.shape, array.dtype)


def mirrored(lon):
    lons = lax.axis_size("lon")
    across = 4 if lons % 4 == 0 else 1
    return (lons // across - 1 - lon // across) * across + lon % across


def straight(lon):
    return lon


def eastward(lon):
    return (lon + 1) % lax.axis_size("lon")


def mirrored_eastward(lon):
    return mirrored(eastward(lon))


def send(block, sections, steps, source_at, target_at):
    lons, lats = lax.axis_size("lon"), lax.axis_size("lat")
    route = []
    for lon in range(lons):
        for lat in range(lats):
            here = source_at(lon) * lats + lat
            there = target_at((lon + steps[1]) % lons) * lats + (lat + steps[0]) % lats
            route.append((here * 2 + sections[0], there * 2 + sections[1]))
    return lax.ppermute(block, AXES, route)


def to_shifted(quarters, source_at, target_at):
    moved = [
        send(quarters[q], (0, 1), (q // 2 - 1, q % 2 - 1), source_at, target_at) for q in range(4)
    ]
    return [moved[3 - q] for q in range(4)]


def body(
    inputs,
    ln_gain,
    ln_shift,
    qkv_weight,
    qkv_bias,
    proj_weight,
    fc1_weight,
    fc1_bias,
    fc2_weight,
    out_bias,
    bias_table,
):
    params = (
        ln_gain,
        ln_shift,
        qkv_weight,
        qkv_bias,
        proj_weight,
        fc1_weight,
        fc1_bias,
        fc2_weight,
        out_bias,
    )
    params = (*params[:7], fc2_weight.transpose(0, 2, 1), out_bias)
    patch = inputs.transpose(0, 2, 3, 1, 4)
    table = bias_table.transpose(0, 2, 3, 1, 4)
    other = send(patch, (1, 0), (0, 0), straight, mirrored)
    arrange = jnp.asarray(arrange_matrix())
    spread = jnp.asarray(spread_matrix())
    addend_shape = jax.ShapeDtypeStruct((2, 2 * HEADS * WIN, 128), jnp.float32)
    bias_scratch = [
        held(table),
        held(spread),
        pltpu.VMEM((24, table.shape[-1]), jnp.float32),
        pltpu.VMEM((12 * 24, spread.shape[0]), jnp.float32),
    ]
    brought = [jax.ShapeDtypeStruct(member.shape, member.dtype) for member in params]
    made = call(
        functools.partial(first_kernel, True),
        (patch, arrange, *params, table, spread),
        "h" * 13,
        [*QUARTERS, addend_shape, jax.ShapeDtypeStruct(arrange.shape, arrange.dtype), *brought],
        [*BLOCK_SCRATCH, held(patch), *bias_scratch, pltpu.SemaphoreType.DMA((13,))],
        BLOCK_FLOPS,
    )
    own_first, (addend_one, arranging), params_one = made[:4], made[4:6], made[6:]
    own_shifted = to_shifted(own_first, straight, mirrored_eastward)
    addend_two, *params_two = call(
        prepare_kernel,
        (table, spread, *params, own_first[0]),
        "h" * 11 + "v",
        [addend_shape, *brought],
        [*bias_scratch, pltpu.SemaphoreType.DMA((11,))],
        200_000_000,
    )
    other_first = call(
        functools.partial(first_kernel, False),
        (other, arranging, *params_one, addend_one),
        "v" * 12,
        QUARTERS,
        BLOCK_SCRATCH,
        BLOCK_FLOPS,
    )
    other_shifted = to_shifted(other_first, mirrored, eastward)
    block_two = functools.partial(
        call,
        second_kernel,
        places="v" * 14,
        outs=QUARTERS,
        scratch=BLOCK_SCRATCH,
        flops=BLOCK_FLOPS,
    )
    own_done = block_two((*own_shifted, *params_two, addend_two))
    own_back = [
        send(own_done[3 - q], (1, 0), (1 - q // 2, 1 - q % 2), mirrored_eastward, straight)
        for q in range(4)
    ]
    other_done = block_two((*other_shifted, *params_two, addend_two))
    across, along, upward = [
        send(other_done[3 - q], (1, 1), (1 - q // 2, 1 - q % 2), eastward, straight)
        for q in (1, 3, 0)
    ]
    placed = call(
        place_kernel,
        (*own_back, across, along, upward, other_done[1], jnp.asarray(place_matrix())),
        "v" * 9,
        jax.ShapeDtypeStruct(patch.shape, patch.dtype),
        [pltpu.VMEM((2 * WIN, C), jnp.float32)],
        1_000_000,
    )
    return placed.transpose(0, 3, 1, 2, 4)


def solution(mesh):
    return jax.shard_map(
        body,
        mesh=mesh,
        in_specs=(
            P("section", None, "lat", "lon", None),
            P("section", None, None),
            P("section", None, None),
            P("section", None, None),
            P("section", None),
            P("section", None, None),
            P("section", None, None),
            P("section", None),
            P("section", None, None),
            P("section", None, None),
            P("section", None, "lat", None, None),
        ),
        out_specs=P("section", None, "lat", "lon", None),
        check_vma=False,
    )
```
